128 devices in a mesh: blk: 16 (over z, y_lo, core), grp: 8 (over y_hi, x).
Axes of the slice: x: 4, y: 4 (y_hi: 2, y_lo: 2; y = y_hi * 2 + y_lo), z: 4, core: 2. Of those that a mesh axis runs over, the one named last changes fastest.
Arguments:
- ratings: bfloat16 [2, 16, 8, 64, 256, 256], P(None, 'blk', 'grp'), may hold values from -6 to 6
- row_index: int32 [2, 16, 8, 64], P(None, 'blk', 'grp'), may hold values from 0 to 7
- col_index: int32 [2, 16, 8, 64], P(None, 'blk', 'grp'), may hold values from 0 to 63
- row_mask: int32 [2, 16, 8, 64, 256], P(None, 'blk', 'grp'), may hold values 0 or 1
- counts: int32 [2, 16, 8], P(None, 'blk', 'grp'), may hold values from 21 to 64, as said below
- owner_list: int32 [2, 16], P(None, 'blk'), may hold values from 0 to 7
- user_factors: float32 [262144, 128], P(('blk', 'grp'))
- item_factors: float32 [262144, 128], P('blk'), may hold values from -2 to 2
Outputs:
- user_final: float32 [262144, 128], P(('blk', 'grp'))
- item_final: float32 [262144, 128], P(('blk', 'grp'))
The draws below stay inside these ranges and needn't reach their ends.
Inputs may be any that keep to these rules, and one draw needn't show every extreme that they name: `counts`: in every sub-epoch some device has exactly 64 live slots, and every device has at least a third of 64, rounded down.
All inputs are finite; a program needn't handle non-finite values. No bound on the sum of `row_mask` on one device may be relied on, other than what follows from the above.
Results may differ from the reference program's by a relative error of at most 0.02.
Values may be sent and summed in bfloat16 or wider, within the bound.
A program may use at most 128 MiB of HBM per device.

```python
import jax
import jax.numpy as jnp
from jax import lax

RANK = 128
TILE = 256
UT_DEV = 8
ITEM_BLK = 16384
TMAX = 64
SUB = 2
BLOCKS = 16
MEMBERS = 8
USR_DEV = 2048
USERS = 262144
ITEMS = 262144
COLT = 64


def draw_counts(key, part):
    key = jax.random.fold_in(key, 2)
    first, second = jax.random.split(key)
    values = jax.random.randint(first, (SUB, BLOCKS * MEMBERS), TMAX // 3, TMAX + 1)
    chosen = jax.random.randint(second, (SUB, 1), 0, BLOCKS * MEMBERS)
    places = jnp.arange(BLOCKS * MEMBERS, dtype=jnp.int32)[None, :]
    values = jnp.where(places == chosen, TMAX, values)
    return values.reshape(SUB, BLOCKS, MEMBERS).astype(jnp.int32)


def draw_user_factors(key, part):
    key = jax.random.fold_in(key, 5)
    first, second = jax.random.split(key)
    low_log = jnp.log(0.1)
    high_log = jnp.log(0.8)
    values = jax.random.normal(second, (USERS, RANK), jnp.float32)
    scales = jnp.exp(jax.random.uniform(first, (USERS // TILE, 1, 1), jnp.float32, low_log, high_log))
    values = values.reshape(USERS // TILE, TILE, RANK) * scales
    return values.reshape(USERS, RANK).astype(jnp.float32)


def touch_ends(entries, stream_key, smallest, high):
    dims = entries.shape
    spot = [jax.random.randint(jax.random.fold_in(stream_key, axis), (), 0, dims[axis]) for axis in range(len(dims))]
    entries = entries.at[tuple(spot)].set(smallest)
    longest = dims.index(max(dims))
    spot[longest] = (spot[longest] + 1) % dims[longest]
    return entries.at[tuple(spot)].set(high)


def block_scale(stream_key, extent, cuts, least, high):
    gain = 1.0
    for dim, shards_of in cuts:
        heights = jax.random.uniform(jax.random.fold_in(jax.random.fold_in(stream_key, 6), dim), (shards_of,), jnp.float32, least / len(cuts), high / len(cuts))
        gain = gain * jnp.repeat(jnp.exp(heights), extent[dim] // shards_of).reshape((-1,) + (1,) * (len(extent) - 1 - dim))
    return gain


def gaussian(own_key, dims, width, most, cuts=(), held_as=jnp.bfloat16):
    array = width * jax.random.normal(own_key, dims, jnp.float32)
    if cuts:
        array = array * block_scale(own_key, dims, cuts, -0.22, 0.18)
    return jnp.clip(array, -most, most).astype(held_as)


def setup_inputs(seed: int = 0) -> dict:
    key_of = jax.random.split(jax.random.key(seed), 9)
    return {
        "ratings": gaussian(key_of[0], (SUB, BLOCKS, MEMBERS, TMAX, TILE, TILE), 1.0, 6.0, ((1, 16), (2, 8))),
        "row_index": touch_ends(jax.random.randint(key_of[1], (SUB, BLOCKS, MEMBERS, TMAX), 0, UT_DEV), jax.random.fold_in(key_of[1], 1), 0, UT_DEV - 1).astype(jnp.int32),
        "col_index": touch_ends(jax.random.randint(key_of[2], (SUB, BLOCKS, MEMBERS, TMAX), 0, COLT), jax.random.fold_in(key_of[2], 1), 0, COLT - 1).astype(jnp.int32),
        "row_mask": touch_ends((jax.random.randint(key_of[3], (SUB, BLOCKS, MEMBERS, TMAX, TILE), 0, 8) < 7).astype(jnp.int32), jax.random.fold_in(key_of[3], 1), 0, 1),
        "counts": draw_counts(jax.random.fold_in(key_of[8], 71), 0),
        "owner_list": touch_ends(jax.random.randint(key_of[5], (SUB, BLOCKS), 0, MEMBERS), jax.random.fold_in(key_of[5], 1), 0, MEMBERS - 1).astype(jnp.int32),
        "user_factors": draw_user_factors(jax.random.fold_in(key_of[8], 71), 0),
        "item_factors": gaussian(key_of[7], (ITEMS, RANK), 0.3, 2.0, ((0, 16),), jnp.float32),
    }


LEARN = 0.004
GRAM = 256.0
RIDGE = 1.0


def device_grads(user_tiles, item_tiles, tile_vals, rows_in, cols_in, mask_in, live_count):
    zero_user = jnp.zeros((UT_DEV, TILE, RANK), jnp.float32)
    zero_item = jnp.zeros((COLT, TILE, RANK), jnp.float32)

    def tile_step(carry, slot):
        grad_user, grad_item = carry
        row_tile = rows_in[slot]
        col_tile = cols_in[slot]
        user_part = user_tiles[row_tile]
        item_part = item_tiles[col_tile]
        predicted = jnp.dot(user_part, item_part.T, preferred_element_type=jnp.float32)
        weights = mask_in[slot].astype(jnp.float32)[:, None]
        errors = (weights * (predicted - tile_vals[slot].astype(jnp.float32))).astype(jnp.bfloat16)
        live = (slot < live_count).astype(jnp.float32)
        grad_user = grad_user.at[row_tile].add(live * jnp.dot(errors, item_part, preferred_element_type=jnp.float32))
        grad_item = grad_item.at[col_tile].add(live * jnp.dot(errors.T, user_part, preferred_element_type=jnp.float32))
        return (grad_user, grad_item), None

    (grad_user, grad_item), _ = lax.scan(tile_step, (zero_user, zero_item), jnp.arange(TMAX, dtype=jnp.int32))
    return grad_user, grad_item


def reference(ratings, row_index, col_index, row_mask, counts, owner_list, user_factors, item_factors):
    user_state = user_factors.reshape(BLOCKS, MEMBERS, USR_DEV, RANK)
    item_state = item_factors.reshape(BLOCKS, ITEM_BLK, RANK)
    identity = jnp.eye(RANK, dtype=jnp.float32)
    for epoch in range(SUB):
        current = jnp.roll(item_state, epoch, axis=0)

        def per_block(block_id):
            user_blk = user_state[block_id]
            item_blk = current[block_id]
            item_bf = item_blk.astype(jnp.bfloat16)
            user_bf = user_blk.astype(jnp.bfloat16)
            item_tiles = item_bf.reshape(COLT, TILE, RANK)

            def per_member(member):
                grad_user, grad_item = device_grads(
                    user_bf[member].reshape(UT_DEV, TILE, RANK), item_tiles,
                    ratings[epoch, block_id, member], row_index[epoch, block_id, member],
                    col_index[epoch, block_id, member], row_mask[epoch, block_id, member],
                    counts[epoch, block_id, member])
                return grad_user.reshape(USR_DEV, RANK), grad_item.reshape(ITEM_BLK, RANK).astype(jnp.bfloat16)

            user_grads, item_parts = lax.map(per_member, jnp.arange(MEMBERS, dtype=jnp.int32))
            owner_rows = user_bf[owner_list[epoch, block_id]]
            owner_gram = jnp.dot(owner_rows.T, owner_rows, preferred_element_type=jnp.float32) * (GRAM / USR_DEV) + RIDGE * identity
            item_gram = jnp.dot(item_bf.T, item_bf, preferred_element_type=jnp.float32) * (GRAM / ITEM_BLK) + RIDGE * identity
            user_pull = jnp.einsum("mur,rq->muq", user_blk, item_gram, precision=lax.Precision.HIGHEST)
            new_user = user_blk - LEARN * (user_grads + user_pull)
            item_grad = jnp.sum(item_parts.astype(jnp.float32), axis=0)
            item_pull = jnp.dot(item_blk, owner_gram, precision=lax.Precision.HIGHEST)
            new_item = item_blk - LEARN * (item_grad + item_pull)
            return new_user, new_item

        user_state, current = lax.map(per_block, jnp.arange(BLOCKS, dtype=jnp.int32))
        item_state = jnp.roll(current, -epoch, axis=0)
    user_final = user_state.reshape(USERS, RANK)
    item_final = jnp.roll(item_state, SUB, axis=0).reshape(ITEMS, RANK)
    return user_final, item_final
```

```python
import functools

import jax
import jax.numpy as jnp
from jax import lax
from jax.experimental import pallas as pl
from jax.experimental.pallas import tpu as pltpu
from jax.sharding import PartitionSpec as P

LEARN = 0.004
GRAM = 256.0
RIDGE = 1.0

TILE = 256
RANK = 128
SLOTS = 64
USER_TILES = 8
ITEM_TILES = 64
OWNERS = 8
GROUP = 4

SUM_ROWS = 1024
SUM_P = 576
SUM_Q = SUM_ROWS - SUM_P
OUT_ROWS = 2048
OUT_P = 1152
OUT_Q = OUT_ROWS - OUT_P
STEP = 32

F32, BF16, I32 = jnp.float32, jnp.bfloat16, jnp.int32
MESH = pl.DeviceIdType.MESH


def dot(a, b, ca=1, cb=0, precision=None):
    return lax.dot_general(
        a, b, (((ca,), (cb,)), ((), ())), precision=precision, preferred_element_type=F32
    )


def ridge():
    row = lax.broadcasted_iota(I32, (RANK, RANK), 0)
    col = lax.broadcasted_iota(I32, (RANK, RANK), 1)
    return jnp.where(row == col, RIDGE, 0.0).astype(F32)


def grads_kernel(
    epoch, rows, cols, counts, ratings, mask, users, items, part_out, users_out, gram_out,
    order, tally, rbuf, vbuf, err, part, acc, ub, ubt, ug, gram, rsem, vsem, osem,
):
    live_count = counts[epoch]
    items_in = pltpu.make_async_copy(items, vbuf, vsem)
    items_in.start()

    def key(t):
        return jnp.where(t < live_count, cols[epoch, t], ITEM_TILES)

    @pl.loop(0, ITEM_TILES + 1)
    def _(j):
        tally[j] = 0

    @pl.loop(0, SLOTS)
    def _(t):
        tally[key(t)] = tally[key(t)] + 1

    def running(j, total):
        here = tally[j]
        tally[j] = total
        return total + here

    lax.fori_loop(0, ITEM_TILES + 1, running, 0)

    @pl.loop(0, SLOTS)
    def _(t):
        place = tally[key(t)]
        tally[key(t)] = place + 1
        order[place] = t
        pltpu.make_async_copy(ratings.at[epoch, t], rbuf.at[place], rsem.at[place]).start()

    for i in range(USER_TILES):
        u = users[pl.ds(i * TILE, TILE), :]
        ub[i] = u.astype(BF16)
        ubt[i] = u.T.astype(BF16)
    own = jnp.zeros((RANK, RANK), F32)
    for i in range(USER_TILES):
        own = own + dot(ubt[i], ub[i])
    gram_out[...] = (own * (GRAM / OUT_ROWS) + ridge()).astype(BF16)

    @pl.loop(0, ITEM_TILES)
    def _(j):
        part[j] = jnp.zeros((RANK, TILE), BF16)

    ug[...] = jnp.zeros_like(ug)
    acc[...] = jnp.zeros_like(acc)
    gram[...] = jnp.zeros_like(gram)
    items_in.wait()

    def errors(p):
        t = order[p]
        pltpu.make_async_copy(ratings.at[epoch, 0], rbuf.at[p], rsem.at[p]).wait()
        predicted = dot(ub[rows[epoch, t]], vbuf[cols[epoch, t]].astype(BF16), 1, 1)
        err[p] = (predicted - rbuf[p].astype(F32)).astype(BF16)

    def weights(t):
        live = jnp.where(t < live_count, 1.0, 0.0)
        return mask[epoch, pl.ds(t, 1), :].astype(F32) * live

    def item_side(p, before):
        t = order[p]
        j = key(t)
        add = dot(ubt[rows[epoch, t]] * weights(t).astype(BF16), err[p])
        total = acc[...] * jnp.where(j == before, 1.0, 0.0) + add
        acc[...] = total
        part[j] = total.astype(BF16)
        return j

    def user_side(p):
        t = order[p]
        i = rows[epoch, t]
        add = dot(vbuf[cols[epoch, t]].astype(BF16), err[p], 0, 1)
        ug[i] = ug[i] + add * weights(t)

    def gram_side(j):
        v = vbuf[j].astype(BF16)
        gram[...] += dot(v, v, 0, 0)

    for q in range(GROUP):
        errors(q)

    def step(g, before):
        for q in range(GROUP):
            before = item_side(g * GROUP + q, before)
        for q in range(GROUP):
            user_side(g * GROUP + q)
        for q in range(GROUP):
            errors(g * GROUP + GROUP + q)
        for q in range(GROUP):
            gram_side(g * GROUP + q)
        return before

    before = lax.fori_loop(0, SLOTS // GROUP - 1, step, -1)
    for q in range(GROUP):
        before = item_side(SLOTS - GROUP + q, before)
    out = pltpu.make_async_copy(part.at[pl.ds(0, ITEM_TILES)], part_out, osem)
    out.start()
    for q in range(GROUP):
        user_side(SLOTS - GROUP + q)
        gram_side(SLOTS - GROUP + q)
    pull = gram[...] * (GRAM / (ITEM_TILES * TILE)) + ridge()

    @pl.loop(0, USER_TILES)
    def _(i):
        u = users[pl.ds(i * TILE, TILE), :]
        pulled = dot(u, pull, precision=lax.Precision.HIGHEST)
        users_out[pl.ds(i * TILE, TILE), :] = u - LEARN * (ug[i].T + pulled)

    out.wait()


def grads(epoch, rows, cols, counts, ratings, mask, users, items):
    smem = pl.BlockSpec(memory_space=pltpu.SMEM)
    vmem = pl.BlockSpec(memory_space=pltpu.VMEM)
    anywhere = pl.BlockSpec(memory_space=pl.ANY)
    dma = pltpu.SemaphoreType.DMA
    return pl.pallas_call(
        functools.partial(grads_kernel, epoch),
        out_shape=[
            jax.ShapeDtypeStruct((ITEM_TILES, RANK, TILE), BF16),
            jax.ShapeDtypeStruct(users.shape, F32),
            jax.ShapeDtypeStruct((RANK, RANK), BF16),
        ],
        in_specs=[smem, smem, smem, anywhere, vmem, vmem, anywhere],
        out_specs=[anywhere, vmem, vmem],
        scratch_shapes=[
            pltpu.SMEM((SLOTS,), I32),
            pltpu.SMEM((ITEM_TILES + 1,), I32),
            pltpu.VMEM((SLOTS, TILE, TILE), BF16),
            pltpu.VMEM((ITEM_TILES, TILE, RANK), items.dtype),
            pltpu.VMEM((SLOTS, TILE, TILE), BF16),
            pltpu.VMEM((ITEM_TILES + 1, RANK, TILE), BF16),
            pltpu.VMEM((RANK, TILE), F32),
            pltpu.VMEM((USER_TILES, TILE, RANK), BF16),
            pltpu.VMEM((USER_TILES, RANK, TILE), BF16),
            pltpu.VMEM((USER_TILES, RANK, TILE), F32),
            pltpu.VMEM((RANK, RANK), F32),
            dma((SLOTS,)),
            dma,
            dma,
        ],
        compiler_params=pltpu.CompilerParams(vmem_limit_bytes=48 * 2**20),
        name="grads%d" % epoch,
    )(rows, cols, counts, ratings, mask, users, items)


def places():
    b, g = lax.axis_index("blk"), lax.axis_index("grp")
    blocks = lax.axis_size("blk")
    x, yh = g % 4, g // 4
    xp, xm, xo, yo = (x + 1) % 4, (x + 3) % 4, (x + 2) % 4, 1 - yh
    x1 = x + 1 - 2 * (x % 2)
    return dict(
        b=b, g=g, x=x, yh=yh, xp=xp, xm=xm, xo=xo, yo=yo,
        to_xp=(b, yh * 4 + xp), to_xm=(b, yh * 4 + xm), to_xo=(b, yh * 4 + xo),
        to_x1=(b, yh * 4 + x1), to_y=(b, yo * 4 + x),
        to_next=((b + 1) % blocks, g), to_last=((b + blocks - 1) % blocks, g),
    )


def add_rows(count, fn):
    @pl.loop(0, count // STEP)
    def _(k):
        fn(pl.ds(pl.multiple_of(k * STEP, STEP), STEP))


class Copies:
    def __init__(self, send, recv):
        self.send, self.recv, self.made = send, recv, []

    def start(self, src, dst, to):
        k = len(self.made)
        copy = pltpu.make_async_remote_copy(
            src_ref=src, dst_ref=dst, send_sem=self.send.at[k], recv_sem=self.recv.at[k],
            device_id=to, device_id_type=MESH,
        )
        copy.start()
        self.made.append(copy)
        return copy

    def finish(self):
        for copy in self.made:
            copy.wait_send()


COPIES = 45


def exchange_kernel(
    epoch, last, owner, part, gram_in, items, out,
    r1p, r1m, r2p, r2m, rq, q1p, q1m, q2p, q2m, ry, gsend, grecv, base, total, newv, landing, send, recv,
):
    w = places()
    x, yh, xp, xm, xo, yo = (w[k] for k in ("x", "yh", "xp", "xm", "xo", "yo"))
    barrier = pltpu.get_barrier_semaphore()
    peers = ("to_xp", "to_xm", "to_xo", "to_y", "to_next", "to_last")
    for peer in peers:
        pl.semaphore_signal(barrier, inc=1, device_id=w[peer], device_id_type=MESH)
    gsend[0] = jnp.where(owner[epoch] == w["g"], gram_in[...], jnp.zeros_like(gram_in))
    pl.semaphore_wait(barrier, len(peers))
    copies = Copies(send, recv)
    half_p, half_q = SUM_P // 2, SUM_Q // 2
    pa, pb = pl.ds(0, half_p), pl.ds(half_p, half_p)
    p_rows, q_rows = pl.ds(0, SUM_P), pl.ds(SUM_P, SUM_Q)

    def own(a, b):
        return a * 4 + b

    c_g0 = copies.start(gsend.at[0], grecv.at[0], w["to_y"])
    c_1p = [copies.start(part.at[own(a, xo), pa], r1p.at[a], w["to_xp"]) for a in range(2)]
    c_1m = [copies.start(part.at[own(a, xo), pb], r1m.at[a], w["to_xm"]) for a in range(2)]
    c_q = [copies.start(part.at[own(yo, d), q_rows], rq.at[d], w["to_y"]) for d in (xo, xp, xm, x)]
    c_2pb = [copies.start(part.at[own(a, xp), pb], r2p.at[a, pb], w["to_xp"]) for a in range(2)]
    c_2ma = [copies.start(part.at[own(a, xm), pa], r2m.at[a, pa], w["to_xm"]) for a in range(2)]

    c_2pa, c_2mb = [], []
    for a in range(2):
        c_1p[a].wait_recv()

        def fn(s, a=a):
            r1p[a, s, :] = (r1p[a, s, :].astype(F32) + part[own(a, xp), s, :].astype(F32)).astype(BF16)

        add_rows(half_p, fn)
        c_2pa.append(copies.start(r1p.at[a], r2p.at[a, pa], w["to_xp"]))
        c_1m[a].wait_recv()

        def fn(s, a=a):
            t = pl.ds(pl.multiple_of(s.start + half_p, STEP), STEP)
            r1m[a, s, :] = (r1m[a, s, :].astype(F32) + part[own(a, xm), t, :].astype(F32)).astype(BF16)

        add_rows(half_p, fn)
        c_2mb.append(copies.start(r1m.at[a], r2m.at[a, pb], w["to_xm"]))

    c_g0.wait_recv()
    gsend[1] = gsend[0] + grecv[0]
    c_g1 = copies.start(gsend.at[1], grecv.at[1], w["to_x1"])

    def sum_q(d):
        def fn(s):
            t = pl.ds(pl.multiple_of(s.start + SUM_P, STEP), STEP)
            rq[d, s, :] = (rq[d, s, :].astype(F32) + part[own(yh, d), t, :].astype(F32)).astype(BF16)

        add_rows(SUM_Q, fn)

    qa, qb = pl.ds(0, half_q), pl.ds(half_q, half_q)
    c_q[0].wait_recv()
    sum_q(xo)
    c_q1p = copies.start(rq.at[xo, qa], q1p, w["to_xp"])
    c_q1m = copies.start(rq.at[xo, qb], q1m, w["to_xm"])
    c_g1.wait_recv()
    gsend[2] = gsend[1] + grecv[1]
    c_g2 = copies.start(gsend.at[2], grecv.at[2], w["to_xo"])
    c_q[1].wait_recv()
    sum_q(xp)
    c_q2pb = copies.start(rq.at[xp, qb], q2p.at[qb], w["to_xp"])
    c_q[2].wait_recv()
    sum_q(xm)
    c_q2ma = copies.start(rq.at[xm, qa], q2m.at[qa], w["to_xm"])

    def sum_p(a):
        def fn(s):
            both = r2p[a, s, :].astype(F32) + r2m[a, s, :].astype(F32)
            return both + part[own(a, x), s, :].astype(F32)

        return fn

    for a in range(2):
        c_2pb[a].wait_recv()
        c_2ma[a].wait_recv()
        c_2pa[a].wait_recv()
        c_2mb[a].wait_recv()
    other, mine = sum_p(yo), sum_p(yh)

    def fn(s):
        r2p[yo, s, :] = other(s).astype(BF16)

    add_rows(SUM_P, fn)
    c_y = copies.start(r2p.at[yo], ry, w["to_y"])

    c_q1p.wait_recv()

    def fn(s):
        q1p[s, :] = (q1p[s, :].astype(F32) + rq[xp, s, :].astype(F32)).astype(BF16)

    add_rows(half_q, fn)
    c_q2pa = copies.start(q1p, q2p.at[qa], w["to_xp"])
    c_q1m.wait_recv()

    def fn(s):
        t = pl.ds(pl.multiple_of(s.start + half_q, STEP), STEP)
        q1m[s, :] = (q1m[s, :].astype(F32) + rq[xm, t, :].astype(F32)).astype(BF16)

    add_rows(half_q, fn)
    c_q2mb = copies.start(q1m, q2m.at[qb], w["to_xm"])

    c_q[3].wait_recv()
    sum_q(x)
    c_g2.wait_recv()
    pull = (gsend[2] + grecv[2]).astype(F32)

    @pl.loop(0, OUT_ROWS // TILE)
    def _(k):
        s = pl.ds(pl.multiple_of(k * TILE, TILE), TILE)
        v = items[s, :].astype(F32)
        base[s, :] = v - LEARN * dot(v, pull, precision=lax.Precision.HIGHEST)

    def fn(s):
        total[s, :] = mine(s)

    add_rows(SUM_P, fn)
    c_y.wait_recv()

    def fn(s):
        total[s, :] = total[s, :] + ry[s, :].astype(F32)

    add_rows(SUM_P, fn)
    for c in (c_q2pb, c_q2ma, c_q2pa, c_q2mb):
        c.wait_recv()

    def fn(s):
        t = pl.ds(pl.multiple_of(s.start + SUM_P, STEP), STEP)
        total[t, :] = rq[x, s, :].astype(F32) + (q2p[s, :].astype(F32) + q2m[s, :].astype(F32))

    add_rows(SUM_Q, fn)

    def update(k):
        s = pl.ds(k * TILE, TILE)
        newv[s, :] = (base[s, :] - LEARN * total[pl.ds(k * RANK, RANK), :].T).astype(BF16)

    for k in range(OUT_ROWS // TILE):
        update(k)
    if last:
        c_v = copies.start(newv, landing, w["to_next"])
        c_v.wait_recv()

        @pl.loop(0, OUT_ROWS // TILE)
        def _(k):
            s = pl.ds(pl.multiple_of(k * TILE, TILE), TILE)
            out[s, :] = landing[s, :].astype(F32)

        copies.finish()
        return

    half_p, half_q = OUT_P // 2, OUT_Q // 2
    p, pa, pb = pl.ds(0, OUT_P), pl.ds(0, half_p), pl.ds(half_p, half_p)
    q, qa, qb = pl.ds(OUT_P, OUT_Q), pl.ds(OUT_P, half_q), pl.ds(OUT_P + half_q, half_q)
    me = w["g"]
    c_vp = copies.start(newv.at[p], out.at[me, p], w["to_next"])
    c_vq = copies.start(newv.at[q], out.at[me, q], w["to_next"])

    def along(o, rows, to):
        return copies.start(out.at[o, rows], out.at[o, rows], w[to])

    c_vp.wait_recv()
    c_py = along(me, p, "to_y")
    c_pp = [along(me, p, "to_xp")]
    c_pm = [along(me, p, "to_xm")]
    c_vq.wait_recv()
    c_qp = along(me, q, "to_xp")
    c_qm = along(me, q, "to_xm")
    c_qy = [along(me, q, "to_y")]
    c_py.wait_recv()
    c_pp.append(along(own(yo, x), p, "to_xp"))
    c_pm.append(along(own(yo, x), p, "to_xm"))
    c_pp[0].wait_recv()
    c_fp = [along(own(yh, xm), pa, "to_xp")]
    c_pm[0].wait_recv()
    c_fm = [along(own(yh, xp), pb, "to_xm")]
    c_qp.wait_recv()
    c_qy.append(along(own(yh, xm), q, "to_y"))
    c_qfp = along(own(yh, xm), qa, "to_xp")
    c_qm.wait_recv()
    c_qy.append(along(own(yh, xp), q, "to_y"))
    c_qfm = along(own(yh, xp), qb, "to_xm")
    c_pp[1].wait_recv()
    c_fp.append(along(own(yo, xm), pa, "to_xp"))
    c_pm[1].wait_recv()
    c_fm.append(along(own(yo, xp), pb, "to_xm"))
    c_qfp.wait_recv()
    c_qfm.wait_recv()
    c_qy.append(along(own(yh, xo), q, "to_y"))
    for c in c_fp + c_fm + c_qy:
        c.wait_recv()
    copies.finish()


def exchange(epoch, last, owner, part, gram, items):
    smem = pl.BlockSpec(memory_space=pltpu.SMEM)
    vmem = pl.BlockSpec(memory_space=pltpu.VMEM)
    dma = pltpu.SemaphoreType.DMA
    if last:
        out = jax.ShapeDtypeStruct((OUT_ROWS, RANK), F32)
    else:
        out = jax.ShapeDtypeStruct((OWNERS, OUT_ROWS, RANK), BF16)

    def wide(*rows):
        return pltpu.VMEM((*rows, TILE), BF16)

    return pl.pallas_call(
        functools.partial(exchange_kernel, epoch, last),
        out_shape=out,
        in_specs=[smem, vmem, vmem, vmem],
        out_specs=vmem,
        scratch_shapes=[
            wide(2, SUM_P // 2), wide(2, SUM_P // 2), wide(2, SUM_P), wide(2, SUM_P),
            wide(4, SUM_Q), wide(SUM_Q // 2), wide(SUM_Q // 2), wide(SUM_Q), wide(SUM_Q), wide(SUM_P),
            pltpu.VMEM((3, RANK, RANK), BF16),
            pltpu.VMEM((3, RANK, RANK), BF16),
            pltpu.VMEM((OUT_ROWS, RANK), F32),
            pltpu.VMEM((SUM_ROWS, TILE), F32),
            pltpu.VMEM((OUT_ROWS, RANK), BF16),
            pltpu.VMEM((OUT_ROWS, RANK), BF16),
            dma((COPIES,)),
            dma((COPIES,)),
        ],
        compiler_params=pltpu.CompilerParams(
            collective_id=epoch, has_side_effects=True, vmem_limit_bytes=48 * 2**20
        ),
        name="exchange%d" % epoch,
    )(owner, part, gram, items)


def local(ratings, row_index, col_index, row_mask, counts, owner_list, user_factors, item_factors):
    epochs = ratings.shape[0]
    ratings = ratings.reshape(epochs, SLOTS, TILE, TILE)
    rows = row_index.reshape(epochs, SLOTS)
    cols = col_index.reshape(epochs, SLOTS)
    mask = row_mask.reshape(epochs, SLOTS, TILE)
    counts = counts.reshape(epochs)
    owner = owner_list.reshape(epochs)
    users = user_factors
    member = lax.axis_index("grp")
    items = item_factors.reshape(ITEM_TILES, TILE, RANK)
    for epoch in range(epochs):
        part, users, gram = grads(epoch, rows, cols, counts, ratings, mask, users, items)
        part = part.reshape(OWNERS, SUM_ROWS, TILE)
        mine = lax.dynamic_slice_in_dim(items.reshape(OWNERS, OUT_ROWS, RANK), member, 1, 0)[0]
        last = epoch == epochs - 1
        moved = exchange(epoch, last, owner, part, gram, mine)
        items = moved if last else moved.reshape(ITEM_TILES, TILE, RANK)
    return users, items


def solution(mesh):
    in_specs = (
        P(None, "blk", "grp", None, None, None),
        P(None, "blk", "grp", None),
        P(None, "blk", "grp", None),
        P(None, "blk", "grp", None, None),
        P(None, "blk", "grp"),
        P(None, "blk"),
        P(("blk", "grp"), None),
        P("blk", None),
    )
    out_specs = (P(("blk", "grp"), None), P(("blk", "grp"), None))
    return jax.shard_map(local, mesh=mesh, in_specs=in_specs, out_specs=out_specs, check_vma=False)
```

```python
import functools

import jax
import jax.numpy as jnp
from jax import lax
from jax.experimental import pallas as pl
from jax.experimental.pallas import tpu as pltpu
from jax.sharding import PartitionSpec as P

LEARN = 0.004
GRAM = 256.0
RIDGE = 1.0

TILE = 256
RANK = 128
SLOTS = 64
USER_TILES = 8
ITEM_TILES = 64
OWNERS = 8
GROUP = 8
USER_ROWS = USER_TILES * TILE

WAVES = 2
HALF = RANK // WAVES
WAVE_ROWS = 8 * HALF
P_ROWS = 288
Q_ROWS = WAVE_ROWS - P_ROWS
PH, QH = P_ROWS // 2, Q_ROWS // 2
UNIT = 16
TILE_UNITS = HALF // UNIT
WAVE_UNITS = WAVE_ROWS // UNIT


def units(owner, start, rows):
    return pl.ds(owner * WAVE_UNITS + start // UNIT, rows // UNIT)


PREV_COL, PREV_ROW, COL, ROW, LAST_COL, LAST_ROW, COUNT, OWNER, TABLE = 0, 64, 128, 192, 256, 320, 328, 329, 384

F32, BF16, I32 = jnp.float32, jnp.bfloat16, jnp.int32
MESH = pl.DeviceIdType.MESH
HIGHEST = lax.Precision.HIGHEST


def dot(a, b, ca=1, cb=0, precision=None):
    return lax.dot_general(
        a, b, (((ca,), (cb,)), ((), ())), precision=precision, preferred_element_type=F32
    )


def ridge():
    row = lax.broadcasted_iota(I32, (RANK, RANK), 0)
    col = lax.broadcasted_iota(I32, (RANK, RANK), 1)
    return jnp.where(row == col, RIDGE, 0.0).astype(F32)


def table_kernel(rows, cols, counts, owner, out):
    for e in range(rows.shape[0]):
        n = counts[e]

        @pl.loop(0, SLOTS, unroll=8)
        def _(t):
            out[e, PREV_COL + t] = SLOTS
            out[e, PREV_ROW + t] = SLOTS
            out[e, LAST_COL + t] = SLOTS
            out[e, COL + t] = cols[e, t]
            out[e, ROW + t] = rows[e, t]

        for i in range(USER_TILES):
            out[e, LAST_ROW + i] = SLOTS
        out[e, COUNT] = n
        out[e, OWNER] = owner[e]

        @pl.loop(0, n)
        def _(t):
            c, r = cols[e, t], rows[e, t]
            out[e, PREV_COL + t] = out[e, LAST_COL + c]
            out[e, LAST_COL + c] = t
            out[e, PREV_ROW + t] = out[e, LAST_ROW + r]
            out[e, LAST_ROW + r] = t


def table(rows, cols, counts, owner):
    smem = pl.BlockSpec(memory_space=pltpu.SMEM)
    return pl.pallas_call(
        table_kernel,
        out_shape=jax.ShapeDtypeStruct((rows.shape[0], TABLE), I32),
        in_specs=[smem] * 4,
        out_specs=smem,
        name="table",
    )(rows, cols, counts, owner)


def places():
    b, g = lax.axis_index("blk"), lax.axis_index("grp")
    blocks = lax.axis_size("blk")
    x, yh = g % 4, g // 4
    xp, xm, xo, yo = (x + 1) % 4, (x + 3) % 4, (x + 2) % 4, 1 - yh
    x1 = x + 1 - 2 * (x % 2)
    return dict(
        b=b, g=g, x=x, yh=yh, xp=xp, xm=xm, xo=xo, yo=yo,
        to_xp=(b, yh * 4 + xp), to_xm=(b, yh * 4 + xm), to_xo=(b, yh * 4 + xo),
        to_x1=(b, yh * 4 + x1), to_y=(b, yo * 4 + x),
        to_next=((b + 1) % blocks, g), to_last=((b + blocks - 1) % blocks, g),
    )


PEERS = ("to_xp", "to_xm", "to_xo", "to_y", "to_next", "to_last")


def in_steps(count, step, fn):
    if count == step:
        fn(0)
        return

    @pl.loop(0, count // step)
    def _(k):
        fn(pl.multiple_of(k * step, step))


class Copies:
    def __init__(self, send, recv):
        self.send, self.recv, self.used, self.open = send, recv, 0, []

    def start(self, src, dst, to):
        k = self.used
        assert k < COPIES
        self.used += 1
        copy = pltpu.make_async_remote_copy(
            src_ref=src, dst_ref=dst, send_sem=self.send.at[k], recv_sem=self.recv.at[k],
            device_id=to, device_id_type=MESH,
        )
        copy.start()
        self.open.append(copy)
        return copy

    def finish(self):
        for copy in self.open:
            copy.wait_send()
        self.open = []


COPIES = 160


class Sum:
    def __init__(self, copies, w, wave, part, bufs, base, total, newv):
        self.c, self.w, self.wave = copies, w, wave
        self.part = part.at[wave]
        self.bufs = {k: v.at[wave] for k, v in bufs.items()}
        self.base, self.total, self.newv = base, total.at[wave], newv.at[wave]

    def start(self):
        w, c, part, b = self.w, self.c, self.part, self.bufs
        xp, xm, xo, yo = w["xp"], w["xm"], w["xo"], w["yo"]
        pa, pb, q = pl.ds(0, PH), pl.ds(PH, PH), pl.ds(P_ROWS, Q_ROWS)
        self.one_p = [c.start(part.at[a * 4 + xo, pa], b["r1p"].at[a], w["to_xp"]) for a in range(2)]
        self.one_m = [c.start(part.at[a * 4 + xo, pb], b["r1m"].at[a], w["to_xm"]) for a in range(2)]
        self.q = [
            c.start(part.at[yo * 4 + d, q], b["rq"].at[d], w["to_y"]) for d in (xo, xp, xm, w["x"])
        ]
        self.two = [c.start(part.at[a * 4 + xp, pb], b["r2p"].at[a, pb], w["to_xp"]) for a in range(2)]
        self.two += [c.start(part.at[a * 4 + xm, pa], b["r2m"].at[a, pa], w["to_xm"]) for a in range(2)]

    def pass_p(self):
        w, c, part, b = self.w, self.c, self.part, self.bufs
        xp, xm = w["xp"], w["xm"]
        pa, pb = pl.ds(0, PH), pl.ds(PH, PH)
        for a in range(2):
            self.one_p[a].wait_recv()

            def fn(k, a=a):
                s = pl.ds(k, 48)
                both = b["r1p"][a, s, :].astype(F32) + part[a * 4 + xp, s, :].astype(F32)
                b["r1p"][a, s, :] = both.astype(BF16)

            in_steps(PH, 48, fn)
            self.two.append(c.start(b["r1p"].at[a], b["r2p"].at[a, pa], w["to_xp"]))
            self.one_m[a].wait_recv()

            def fn(k, a=a):
                s, t = pl.ds(k, 48), pl.ds(k + PH, 48)
                both = b["r1m"][a, s, :].astype(F32) + part[a * 4 + xm, t, :].astype(F32)
                b["r1m"][a, s, :] = both.astype(BF16)

            in_steps(PH, 48, fn)
            self.two.append(c.start(b["r1m"].at[a], b["r2m"].at[a, pb], w["to_xm"]))

    def add_q(self, copy, d):
        part, b, yh = self.part, self.bufs, self.w["yh"]
        copy.wait_recv()

        def fn(k):
            s, t = pl.ds(k, 112), pl.ds(k + P_ROWS, 112)
            both = b["rq"][d, s, :].astype(F32) + part[yh * 4 + d, t, :].astype(F32)
            b["rq"][d, s, :] = both.astype(BF16)

        in_steps(Q_ROWS, 112, fn)

    def far_q(self):
        w, c, b, xo = self.w, self.c, self.bufs, self.w["xo"]
        self.add_q(self.q[0], xo)
        self.q1p = c.start(b["rq"].at[xo, pl.ds(0, QH)], b["q1p"], w["to_xp"])
        self.q1m = c.start(b["rq"].at[xo, pl.ds(QH, QH)], b["q1m"], w["to_xm"])

    def near_q(self):
        w, c, b, xp, xm = self.w, self.c, self.bufs, self.w["xp"], self.w["xm"]
        qa, qb = pl.ds(0, QH), pl.ds(QH, QH)
        self.add_q(self.q[1], xp)
        self.q2 = [c.start(b["rq"].at[xp, qb], b["q2p"].at[qb], w["to_xp"])]
        self.add_q(self.q[2], xm)
        self.q2.append(c.start(b["rq"].at[xm, qa], b["q2m"].at[qa], w["to_xm"]))

    def pass_q(self):
        w, c, b, xp, xm = self.w, self.c, self.bufs, self.w["xp"], self.w["xm"]
        self.q1p.wait_recv()
        b["q1p"][...] = (b["q1p"][...].astype(F32) + b["rq"][xp, pl.ds(0, QH), :].astype(F32)).astype(BF16)
        self.q2.append(c.start(b["q1p"], b["q2p"].at[pl.ds(0, QH)], w["to_xp"]))
        self.q1m.wait_recv()
        b["q1m"][...] = (b["q1m"][...].astype(F32) + b["rq"][xm, pl.ds(QH, QH), :].astype(F32)).astype(BF16)
        self.q2.append(c.start(b["q1m"], b["q2m"].at[pl.ds(QH, QH)], w["to_xm"]))

    def sum_p(self, a, s):
        part, b = self.part, self.bufs
        both = b["r2p"][a, s, :].astype(F32) + b["r2m"][a, s, :].astype(F32)
        return both + part[a * 4 + self.w["x"], s, :].astype(F32)

    def cross_p(self):
        w, b, yo, yh = self.w, self.bufs, self.w["yo"], self.w["yh"]
        for copy in self.two:
            copy.wait_recv()

        def fn(k):
            s = pl.ds(k, 48)
            b["r2p"][yo, s, :] = self.sum_p(yo, s).astype(BF16)

        in_steps(P_ROWS, 48, fn)
        self.y = self.c.start(b["r2p"].at[yo], b["ry"], w["to_y"])

        def fn(k):
            s = pl.ds(k, 48)
            self.total[s, :] = self.sum_p(yh, s)

        in_steps(P_ROWS, 48, fn)

    def finish(self, landing):
        w, b, x, total = self.w, self.bufs, self.w["x"], self.total
        self.add_q(self.q[3], x)
        for copy in self.q2:
            copy.wait_recv()

        def fn(k):
            s, t = pl.ds(k, 112), pl.ds(k + P_ROWS, 112)
            both = b["q2p"][s, :].astype(F32) + b["q2m"][s, :].astype(F32)
            total[t, :] = b["rq"][x, s, :].astype(F32) + both

        in_steps(Q_ROWS, 112, fn)
        self.y.wait_recv()

        def fn(k):
            s = pl.ds(k, 48)
            total[s, :] = total[s, :] + b["ry"][s, :].astype(F32)

        in_steps(P_ROWS, 48, fn)

        @pl.loop(0, OWNERS)
        def _(k):
            s = pl.ds(pl.multiple_of(k * HALF, HALF), HALF)
            old = self.base[k, pl.ds(HALF * self.wave, HALF), :]
            new = (old - LEARN * total[s, :]).astype(BF16)
            for u in range(TILE_UNITS):
                self.newv[k * TILE_UNITS + u] = new[u * UNIT : (u + 1) * UNIT]

        landing, owner = landing
        landing = landing.at[self.wave]
        self.shift = [
            self.c.start(self.newv.at[units(0, at, n)], landing.at[units(owner, at, n)], w["to_next"])
            for at, n in ((0, P_ROWS), (P_ROWS, Q_ROWS))
        ]


class Gather:
    def __init__(self, copies, w, wave, vt):
        self.c, self.w, self.vt = copies, w, vt.at[wave]

    def along(self, owner, rows, to):
        ref = self.vt.at[units(owner, *rows)]
        return self.c.start(ref, ref, self.w[to])

    def first(self, shift):
        me = self.w["g"]
        p, q = (0, P_ROWS), (P_ROWS, Q_ROWS)
        shift[0].wait_recv()
        self.py = self.along(me, p, "to_y")
        self.pp = [self.along(me, p, "to_xp")]
        self.pm = [self.along(me, p, "to_xm")]
        shift[1].wait_recv()
        self.qp = self.along(me, q, "to_xp")
        self.qm = self.along(me, q, "to_xm")
        self.rest = [self.along(me, q, "to_y")]

    def across(self):
        w = self.w
        self.py.wait_recv()
        p = (0, P_ROWS)
        self.pp.append(self.along(w["yo"] * 4 + w["x"], p, "to_xp"))
        self.pm.append(self.along(w["yo"] * 4 + w["x"], p, "to_xm"))

    def forward_p(self, k):
        w = self.w
        row = (w["yh"], w["yo"])[k] * 4
        self.pp[k].wait_recv()
        self.rest.append(self.along(row + w["xm"], (0, PH), "to_xp"))
        self.pm[k].wait_recv()
        self.rest.append(self.along(row + w["xp"], (PH, PH), "to_xm"))

    def forward_q(self):
        w = self.w
        row, q = w["yh"] * 4, (P_ROWS, Q_ROWS)
        self.qp.wait_recv()
        self.qf = [self.along(row + w["xm"], (P_ROWS, QH), "to_xp")]
        self.rest.append(self.along(row + w["xm"], q, "to_y"))
        self.qm.wait_recv()
        self.qf.append(self.along(row + w["xp"], (P_ROWS + QH, QH), "to_xm"))
        self.rest.append(self.along(row + w["xp"], q, "to_y"))

    def across_q(self):
        w = self.w
        for copy in self.qf:
            copy.wait_recv()
        self.rest.append(self.along(w["yh"] * 4 + w["xo"], (P_ROWS, Q_ROWS), "to_y"))

    def finish(self):
        for copy in self.rest:
            copy.wait_recv()


def epochs_kernel(
    idx, ratings, mask_in, users_in, items_in, users_out, items_out,
    users, mask, rbuf, err, stage, vown, acc, ub, ubt, vt0, vt1, part,
    r1p, r1m, r2p, r2m, rq, q1p, q1m, q2p, q2m, ry, gsend, grecv, base, total, newv, landing, final,
    rsem, vsem, lsem, send, recv,
):
    w = places()
    copies = Copies(send, recv)
    chunks = SLOTS // GROUP
    stages = stage.shape[0]
    barrier = pltpu.get_barrier_semaphore()
    for peer in PEERS:
        pl.semaphore_signal(barrier, inc=1, device_id=w[peer], device_id_type=MESH)

    def local_copy(src, dst, k):
        copy = pltpu.make_async_copy(src, dst, lsem.at[k])
        copy.start()
        return copy

    users_here = local_copy(users_in, users, 0)

    def items_here(k):
        copy = pltpu.make_async_copy(
            items_in.at[pl.ds(k * OWNERS, OWNERS)], stage.at[k % stages], vsem.at[k]
        )
        copy.start()
        return copy

    arriving = [items_here(k) for k in range(stages)]
    mask_here = local_copy(mask_in, mask, 1)
    own_here = local_copy(items_in.at[pl.ds(w["g"] * OWNERS, OWNERS)], vown, 2)

    def fetch(e, k):
        s = pl.ds(k * GROUP, GROUP)
        return pltpu.make_async_copy(ratings.at[e, s], rbuf.at[s], rsem.at[k])

    def prepare_users(e, first):
        own = jnp.zeros((RANK, RANK), F32)
        for i in range(USER_TILES):
            u = users[pl.ds(i * TILE, TILE), :]
            ub[i] = u.astype(BF16)
            ut = u.T.astype(BF16)
            ubt[0, i], ubt[1, i] = ut[:HALF], ut[HALF:]
            own = own + dot(ut, ub[i])
        own = (own * (GRAM / USER_ROWS) + ridge()).astype(BF16)
        gsend[e, 0] = jnp.where(idx[e, OWNER] == w["g"], own, jnp.zeros_like(own))
        if first:
            pl.semaphore_wait(barrier, len(PEERS))
        return copies.start(gsend.at[e, 0], grecv.at[e, 0], w["to_y"])

    def spread_gram(e, k, copy):
        copy.wait_recv()
        gsend[e, k] = gsend[e, k - 1] + grecv[e, k - 1]
        return copies.start(gsend.at[e, k], grecv.at[e, k], w["to_x1" if k == 1 else "to_xo"])

    def vtile(vt, j):
        first = j * TILE_UNITS
        return jnp.concatenate(
            [vt[wave, first + u] for wave in range(WAVES) for u in range(TILE_UNITS)], axis=0
        )

    def weights(e, t):
        row = mask[e, pl.ds(t, 1), :].astype(F32)
        return jnp.where(t < idx[e, COUNT], row, jnp.zeros_like(row))

    def errors(e, vt, t):
        predicted = dot(ub[idx[e, ROW + t]], vtile(vt, idx[e, COL + t]))
        err[t] = (predicted - rbuf[t].astype(F32)).astype(BF16)

    def item_dot(e, wave, t):
        u = ubt[wave, idx[e, ROW + t]]
        return dot(u * weights(e, t).astype(BF16), err[t])

    def item_add(e, wave, t, add):
        acc[wave, t] = acc[wave, idx[e, PREV_COL + t]] + add

    def item_done(e, wave):
        @pl.loop(0, ITEM_TILES, unroll=4)
        def _(j):
            s = pl.ds(pl.multiple_of(lax.rem(j, OWNERS) * HALF, HALF), HALF)
            part[wave, lax.div(j, OWNERS), s, :] = acc[wave, idx[e, LAST_COL + j]].astype(BF16)

    def first_pass(e, vt):
        fetch(e, 0).wait()
        for q in range(GROUP):
            errors(e, vt, q)

        @pl.loop(0, chunks - 1)
        def _(g):
            adds = [item_dot(e, 0, g * GROUP + q) for q in range(GROUP)]
            fetch(e, g + 1).wait()
            for q in range(GROUP):
                errors(e, vt, (g + 1) * GROUP + q)
            for q in range(GROUP):
                item_add(e, 0, g * GROUP + q, adds[q])

        adds = [item_dot(e, 0, SLOTS - GROUP + q) for q in range(GROUP)]
        for q in range(GROUP):
            item_add(e, 0, SLOTS - GROUP + q, adds[q])
        item_done(e, 0)

    def second_pass(e):
        @pl.loop(0, chunks)
        def _(g):
            adds = [item_dot(e, 1, g * GROUP + q) for q in range(GROUP)]
            for q in range(GROUP):
                item_add(e, 1, g * GROUP + q, adds[q])

        item_done(e, 1)

    def user_pass(e, vt, first, last):
        @pl.loop(first, last)
        def _(g):
            def add_dot(t):
                return dot(vtile(vt, idx[e, COL + t]), err[t], 1, 1) * weights(e, t)

            for h in range(2):
                slots = [g * GROUP + h * (GROUP // 2) + q for q in range(GROUP // 2)]
                adds = [add_dot(t) for t in slots]
                for t, add in zip(slots, adds):
                    before = idx[e, PREV_ROW + t]
                    acc[0, t] = acc[0, before] + add[:HALF]
                    acc[1, t] = acc[1, before] + add[HALF:]

    def item_gram(vt):
        def add(j, gram):
            for q in range(4):
                v = vtile(vt, j * 4 + q)
                gram = gram + dot(v, v, 1, 1)
            return gram

        gram = lax.fori_loop(0, ITEM_TILES // 4, add, jnp.zeros((RANK, RANK), F32))
        return gram * (GRAM / (ITEM_TILES * TILE)) + ridge()

    def user_update(e, pull):
        @pl.loop(0, USER_TILES)
        def _(i):
            s = pl.ds(pl.multiple_of(i * TILE, TILE), TILE)
            u = users[s, :]
            at = idx[e, LAST_ROW + i]
            grad = jnp.concatenate([acc[0, at], acc[1, at]], axis=0)
            users[s, :] = u - LEARN * (grad.T + dot(u, pull, precision=HIGHEST))

    def item_base(e, copy):
        copy.wait_recv()
        pull = (gsend[e, 2] + grecv[e, 2]).astype(F32)

        @pl.loop(0, OWNERS)
        def _(k):
            if e == 0:
                v = vown[k].T
            else:
                v = vtile(vt1, w["g"] * OWNERS + k).astype(F32)
            base[k] = v - LEARN * dot(pull, v, 0, 0, precision=HIGHEST)

    bufs = dict(
        r1p=r1p, r1m=r1m, r2p=r2p, r2m=r2m, rq=rq, q1p=q1p, q1m=q1m, q2p=q2p, q2m=q2m, ry=ry
    )

    def sums(e):
        at = {k: v.at[e] for k, v in bufs.items()}
        return [Sum(copies, w, wave, part, at, base, total, newv) for wave in range(WAVES)]

    users_here.wait()
    gram_copy = prepare_users(0, True)
    zero = jnp.zeros((HALF, TILE), F32)
    acc[0, SLOTS] = zero
    acc[1, SLOTS] = zero
    for k in range(OWNERS):
        arriving[k].wait()

        @pl.loop(0, OWNERS, unroll=2)
        def _(j):
            v = stage[k % stages, j].T.astype(BF16)
            for u in range(TILE_UNITS):
                at = (k * OWNERS + j) * TILE_UNITS + u
                vt0[0, at] = v[u * UNIT : (u + 1) * UNIT]
                vt0[1, at] = v[HALF + u * UNIT : HALF + (u + 1) * UNIT]

        if k + stages < OWNERS:
            arriving.append(items_here(k + stages))
        for c in range(chunks // OWNERS * k, chunks // OWNERS * (k + 1)):
            fetch(0, c).start()
    gram_copy = spread_gram(0, 1, gram_copy)
    mask_here.wait()
    own_here.wait()
    first_pass(0, vt0)
    s0, s1 = sums(0)
    gram_copy = spread_gram(0, 2, gram_copy)
    s0.start()
    for k in range(chunks):
        fetch(1, k).start()
    second_pass(0)
    s0.pass_p()
    s0.far_q()
    s1.start()
    item_base(0, gram_copy)
    s0.near_q()
    s0.pass_q()
    user_pass(0, vt0, 0, 2)
    s0.cross_p()
    s1.pass_p()
    s1.far_q()
    user_pass(0, vt0, 2, 4)
    s0.finish((vt1, w["g"]))
    s1.near_q()
    s1.pass_q()
    g0, g1 = (Gather(copies, w, wave, vt1) for wave in range(WAVES))
    g0.first(s0.shift)
    s1.cross_p()
    user_pass(0, vt0, 4, 6)
    g0.across()
    s1.finish((vt1, w["g"]))
    g0.forward_p(0)
    g0.forward_q()
    g1.first(s1.shift)
    user_pass(0, vt0, 6, 8)
    g0.forward_p(1)
    g0.across_q()
    g1.across()
    pull = item_gram(vt0)
    g1.forward_p(0)
    g1.forward_q()
    user_update(0, pull)
    g1.forward_p(1)
    g1.across_q()
    gram_copy = prepare_users(1, False)
    g0.finish()
    gram_copy = spread_gram(1, 1, gram_copy)
    g1.finish()
    copies.finish()

    first_pass(1, vt1)
    s0, s1 = sums(1)
    gram_copy = spread_gram(1, 2, gram_copy)
    s0.start()
    second_pass(1)
    s0.pass_p()
    s0.far_q()
    s1.start()
    item_base(1, gram_copy)
    s0.near_q()
    s0.pass_q()
    user_pass(1, vt1, 0, 2)
    s0.cross_p()
    s1.pass_p()
    s1.far_q()
    user_pass(1, vt1, 2, 5)
    s0.finish((landing, 0))
    s1.near_q()
    s1.pass_q()
    user_pass(1, vt1, 5, 8)
    s1.cross_p()
    user_update(1, item_gram(vt1))
    users_gone = local_copy(users, users_out, 0)
    s1.finish((landing, 0))
    for copy in s0.shift + s1.shift:
        copy.wait_recv()

    @pl.loop(0, OWNERS)
    def _(k):
        v = vtile(landing, k).astype(F32)
        final[pl.ds(pl.multiple_of(k * TILE, TILE), TILE), :] = v.T

    items_gone = local_copy(final, items_out, 1)
    copies.finish()
    users_gone.wait()
    items_gone.wait()


def epochs(idx, ratings, mask, users, items):
    smem = pl.BlockSpec(memory_space=pltpu.SMEM)
    anywhere = pl.BlockSpec(memory_space=pl.ANY)
    dma = pltpu.SemaphoreType.DMA
    count = ratings.shape[0]

    def wide(*rows):
        return pltpu.VMEM((count, WAVES, *rows, TILE), BF16)

    return pl.pallas_call(
        epochs_kernel,
        out_shape=[jax.ShapeDtypeStruct(users.shape, F32), jax.ShapeDtypeStruct(users.shape, F32)],
        in_specs=[smem, anywhere, anywhere, anywhere, anywhere],
        out_specs=[anywhere, anywhere],
        scratch_shapes=[
            pltpu.VMEM(users.shape, F32),
            pltpu.VMEM(mask.shape, I32),
            pltpu.VMEM((SLOTS, TILE, TILE), BF16),
            pltpu.VMEM((SLOTS, TILE, TILE), BF16),
            pltpu.VMEM((4, OWNERS, TILE, RANK), F32),
            pltpu.VMEM((OWNERS, TILE, RANK), F32),
            pltpu.VMEM((WAVES, SLOTS + 1, HALF, TILE), F32),
            pltpu.VMEM((USER_TILES, TILE, RANK), BF16),
            pltpu.VMEM((WAVES, USER_TILES, HALF, TILE), BF16),
            pltpu.VMEM((WAVES, OWNERS * WAVE_UNITS, UNIT, TILE), BF16),
            pltpu.VMEM((WAVES, OWNERS * WAVE_UNITS, UNIT, TILE), BF16),
            pltpu.VMEM((WAVES, OWNERS, WAVE_ROWS, TILE), BF16),
            wide(2, PH), wide(2, PH), wide(2, P_ROWS), wide(2, P_ROWS),
            wide(4, Q_ROWS), wide(QH), wide(QH), wide(Q_ROWS), wide(Q_ROWS), wide(P_ROWS),
            pltpu.VMEM((count, 3, RANK, RANK), BF16),
            pltpu.VMEM((count, 3, RANK, RANK), BF16),
            pltpu.VMEM((OWNERS, RANK, TILE), F32),
            pltpu.VMEM((WAVES, WAVE_ROWS, TILE), F32),
            pltpu.VMEM((WAVES, WAVE_UNITS, UNIT, TILE), BF16),
            pltpu.VMEM((WAVES, WAVE_UNITS, UNIT, TILE), BF16),
            pltpu.VMEM(users.shape, F32),
            dma((SLOTS // GROUP,)),
            dma((OWNERS,)),
            dma((3,)),
            dma((COPIES,)),
            dma((COPIES,)),
        ],
        compiler_params=pltpu.CompilerParams(
            collective_id=0, has_side_effects=True, vmem_limit_bytes=62 * 2**20
        ),
        name="epochs",
    )(idx, ratings, mask, users, items)


def local(ratings, row_index, col_index, row_mask, counts, owner_list, user_factors, item_factors):
    count = ratings.shape[0]
    idx = table(
        row_index.reshape(count, SLOTS),
        col_index.reshape(count, SLOTS),
        counts.reshape(count),
        owner_list.reshape(count),
    )
    users, items = epochs(
        idx,
        ratings.reshape(count, SLOTS, TILE, TILE),
        row_mask.reshape(count, SLOTS, TILE),
        user_factors,
        item_factors.reshape(ITEM_TILES, TILE, RANK),
    )
    return users, items


def solution(mesh):
    in_specs = (
        P(None, "blk", "grp", None, None, None),
        P(None, "blk", "grp", None),
        P(None, "blk", "grp", None),
        P(None, "blk", "grp", None, None),
        P(None, "blk", "grp"),
        P(None, "blk"),
        P(("blk", "grp"), None),
        P("blk", None),
    )
    out_specs = (P(("blk", "grp"), None), P(("blk", "grp"), None))
    return jax.shard_map(local, mesh=mesh, in_specs=in_specs, out_specs=out_specs, check_vma=False)
```

```python
import functools

import jax
import jax.numpy as jnp
from jax import lax
from jax.experimental import pallas as pl
from jax.experimental.pallas import tpu as pltpu
from jax.sharding import PartitionSpec as P

LEARN = 0.004
GRAM = 256.0
RIDGE = 1.0

TILE = 256
RANK = 128
SLOTS = 64
USER_TILES = 8
ITEM_TILES = 64
OWNERS = 8
GROUP = 8
USER_ROWS = USER_TILES * TILE

WAVES = 2
HALF = RANK // WAVES
WAVE_ROWS = 8 * HALF
P_ROWS = 288
Q_ROWS = WAVE_ROWS - P_ROWS
PH, QH = P_ROWS // 2, Q_ROWS // 2
UNIT = 16
TILE_UNITS = HALF // UNIT
WAVE_UNITS = WAVE_ROWS // UNIT


def units(owner, start, rows):
    return pl.ds(owner * WAVE_UNITS + start // UNIT, rows // UNIT)


PREV_COL, PREV_ROW, LAST_COL, LAST_ROW, LISTS = 0, 1, 2, 3, 4

F32, BF16, I32 = jnp.float32, jnp.bfloat16, jnp.int32
MESH = pl.DeviceIdType.MESH
HIGHEST = lax.Precision.HIGHEST


def dot(a, b, ca=1, cb=0, precision=None):
    return lax.dot_general(
        a, b, (((ca,), (cb,)), ((), ())), precision=precision, preferred_element_type=F32
    )


def ridge():
    row = lax.broadcasted_iota(I32, (RANK, RANK), 0)
    col = lax.broadcasted_iota(I32, (RANK, RANK), 1)
    return jnp.where(row == col, RIDGE, 0.0).astype(F32)


def places():
    b, g = lax.axis_index("blk"), lax.axis_index("grp")
    blocks = lax.axis_size("blk")
    x, yh = g % 4, g // 4
    xp, xm, xo, yo = (x + 1) % 4, (x + 3) % 4, (x + 2) % 4, 1 - yh
    x1 = x + 1 - 2 * (x % 2)
    return dict(
        b=b, g=g, x=x, yh=yh, xp=xp, xm=xm, xo=xo, yo=yo,
        to_xp=(b, yh * 4 + xp), to_xm=(b, yh * 4 + xm), to_xo=(b, yh * 4 + xo),
        to_x1=(b, yh * 4 + x1), to_y=(b, yo * 4 + x),
        to_next=((b + 1) % blocks, g), to_last=((b + blocks - 1) % blocks, g),
    )


PEERS = ("to_xp", "to_xm", "to_xo", "to_y", "to_next", "to_last")


def in_steps(count, step, fn):
    if count == step:
        fn(0)
        return

    @pl.loop(0, count // step)
    def _(k):
        fn(pl.multiple_of(k * step, step))


class Copies:
    def __init__(self, send, recv):
        self.send, self.recv, self.used, self.open = send, recv, 0, []

    def start(self, src, dst, to):
        k = self.used
        assert k < COPIES
        self.used += 1
        copy = pltpu.make_async_remote_copy(
            src_ref=src, dst_ref=dst, send_sem=self.send.at[k], recv_sem=self.recv.at[k],
            device_id=to, device_id_type=MESH,
        )
        copy.start()
        self.open.append(copy)
        return copy

    def finish(self):
        for copy in self.open:
            copy.wait_send()
        self.open = []


COPIES = 160

ORDER_0 = (
    "s0", "B", "p0", "f0", "s1", "I", "n0", "q0", "U", "c0", "p1", "f1", "F0", "a0", "n1", "q1",
    "U", "x0", "c1", "k0", "r0", "U", "F1", "l0", "a1", "z0", "U", "x1", "k1", "r1", "V", "l1", "z1",
)
ORDER_1 = (
    "s0", "B", "p0", "f0", "s1", "I", "n0", "q0", "U", "c0", "p1", "f1", "U", "F0", "n1", "q1", "U", "U", "c1", "V", "O",
    "F1",
)


class Sum:
    def __init__(self, copies, w, wave, part, bufs, base, total, newv):
        self.c, self.w, self.wave = copies, w, wave
        self.part = part.at[wave]
        self.bufs = {k: v.at[wave] for k, v in bufs.items()}
        self.base, self.total, self.newv = base, total.at[wave], newv.at[wave]

    def start(self):
        w, c, part, b = self.w, self.c, self.part, self.bufs
        xp, xm, xo, yo = w["xp"], w["xm"], w["xo"], w["yo"]
        pa, pb, q = pl.ds(0, PH), pl.ds(PH, PH), pl.ds(P_ROWS, Q_ROWS)
        self.rows = rows = (yo, w["yh"])
        self.one_p, self.one_m = [], []
        for a in rows:
            self.one_p.append(c.start(part.at[a * 4 + xo, pa], b["r1p"].at[a], w["to_xp"]))
            self.one_m.append(c.start(part.at[a * 4 + xo, pb], b["r1m"].at[a], w["to_xm"]))
        self.q = [
            c.start(part.at[yo * 4 + d, q], b["rq"].at[d], w["to_y"]) for d in (xo, xp, xm, w["x"])
        ]
        self.two = []
        for a in rows:
            to_p = c.start(part.at[a * 4 + xp, pb], b["r2p"].at[a, pb], w["to_xp"])
            to_m = c.start(part.at[a * 4 + xm, pa], b["r2m"].at[a, pa], w["to_xm"])
            self.two.append([to_p, to_m])

    def pass_p(self):
        w, c, part, b = self.w, self.c, self.part, self.bufs
        xp, xm = w["xp"], w["xm"]
        pa, pb = pl.ds(0, PH), pl.ds(PH, PH)
        for k, a in enumerate(self.rows):
            self.one_p[k].wait_recv()

            def fn(k, a=a):
                s = pl.ds(k, 48)
                both = b["r1p"][a, s, :].astype(F32) + part[a * 4 + xp, s, :].astype(F32)
                b["r1p"][a, s, :] = both.astype(BF16)

            in_steps(PH, 48, fn)
            self.two[k].append(c.start(b["r1p"].at[a], b["r2p"].at[a, pa], w["to_xp"]))
            self.one_m[k].wait_recv()

            def fn(k, a=a):
                s, t = pl.ds(k, 48), pl.ds(k + PH, 48)
                both = b["r1m"][a, s, :].astype(F32) + part[a * 4 + xm, t, :].astype(F32)
                b["r1m"][a, s, :] = both.astype(BF16)

            in_steps(PH, 48, fn)
            self.two[k].append(c.start(b["r1m"].at[a], b["r2m"].at[a, pb], w["to_xm"]))

    def add_q(self, copy, d):
        part, b, yh = self.part, self.bufs, self.w["yh"]
        copy.wait_recv()

        def fn(k):
            s, t = pl.ds(k, 112), pl.ds(k + P_ROWS, 112)
            both = b["rq"][d, s, :].astype(F32) + part[yh * 4 + d, t, :].astype(F32)
            b["rq"][d, s, :] = both.astype(BF16)

        in_steps(Q_ROWS, 112, fn)

    def far_q(self):
        w, c, b, xo = self.w, self.c, self.bufs, self.w["xo"]
        self.add_q(self.q[0], xo)
        self.q1p = c.start(b["rq"].at[xo, pl.ds(0, QH)], b["q1p"], w["to_xp"])
        self.q1m = c.start(b["rq"].at[xo, pl.ds(QH, QH)], b["q1m"], w["to_xm"])

    def near_q(self):
        w, c, b, xp, xm = self.w, self.c, self.bufs, self.w["xp"], self.w["xm"]
        qa, qb = pl.ds(0, QH), pl.ds(QH, QH)
        self.add_q(self.q[1], xp)
        self.q2 = [c.start(b["rq"].at[xp, qb], b["q2p"].at[qb], w["to_xp"])]
        self.add_q(self.q[2], xm)
        self.q2.append(c.start(b["rq"].at[xm, qa], b["q2m"].at[qa], w["to_xm"]))

    def pass_q(self):
        w, c, b, xp, xm = self.w, self.c, self.bufs, self.w["xp"], self.w["xm"]
        self.q1p.wait_recv()
        b["q1p"][...] = (b["q1p"][...].astype(F32) + b["rq"][xp, pl.ds(0, QH), :].astype(F32)).astype(BF16)
        self.q2.append(c.start(b["q1p"], b["q2p"].at[pl.ds(0, QH)], w["to_xp"]))
        self.q1m.wait_recv()
        b["q1m"][...] = (b["q1m"][...].astype(F32) + b["rq"][xm, pl.ds(QH, QH), :].astype(F32)).astype(BF16)
        self.q2.append(c.start(b["q1m"], b["q2m"].at[pl.ds(QH, QH)], w["to_xm"]))

    def sum_p(self, a, s):
        part, b = self.part, self.bufs
        both = b["r2p"][a, s, :].astype(F32) + b["r2m"][a, s, :].astype(F32)
        return both + part[a * 4 + self.w["x"], s, :].astype(F32)

    def cross_p(self):
        w, b, yo, yh = self.w, self.bufs, self.w["yo"], self.w["yh"]
        for copy in self.two[0]:
            copy.wait_recv()

        def fn(k):
            s = pl.ds(k, 48)
            b["r2p"][yo, s, :] = self.sum_p(yo, s).astype(BF16)

        in_steps(P_ROWS, 48, fn)
        self.y = self.c.start(b["r2p"].at[yo], b["ry"], w["to_y"])
        for copy in self.two[1]:
            copy.wait_recv()

        def fn(k):
            s = pl.ds(k, 48)
            self.total[s, :] = self.sum_p(yh, s)

        in_steps(P_ROWS, 48, fn)

    def finish(self, landing):
        w, b, x, total = self.w, self.bufs, self.w["x"], self.total
        self.add_q(self.q[3], x)
        for copy in self.q2:
            copy.wait_recv()

        def fn(k):
            s, t = pl.ds(k, 112), pl.ds(k + P_ROWS, 112)
            both = b["q2p"][s, :].astype(F32) + b["q2m"][s, :].astype(F32)
            total[t, :] = b["rq"][x, s, :].astype(F32) + both

        in_steps(Q_ROWS, 112, fn)
        self.y.wait_recv()

        def fn(k):
            s = pl.ds(k, 48)
            total[s, :] = total[s, :] + b["ry"][s, :].astype(F32)

        in_steps(P_ROWS, 48, fn)

        @pl.loop(0, OWNERS)
        def _(k):
            s = pl.ds(pl.multiple_of(k * HALF, HALF), HALF)
            old = self.base[k, pl.ds(HALF * self.wave, HALF), :]
            new = (old - LEARN * total[s, :]).astype(BF16)
            for u in range(TILE_UNITS):
                self.newv[k * TILE_UNITS + u] = new[u * UNIT : (u + 1) * UNIT]

        landing, owner = landing
        landing = landing.at[self.wave]
        self.shift = [
            self.c.start(self.newv.at[units(0, at, n)], landing.at[units(owner, at, n)], w["to_next"])
            for at, n in ((0, P_ROWS), (P_ROWS, Q_ROWS))
        ]


class Gather:
    def __init__(self, copies, w, wave, vt):
        self.c, self.w, self.vt = copies, w, vt.at[wave]

    def along(self, owner, rows, to):
        ref = self.vt.at[units(owner, *rows)]
        return self.c.start(ref, ref, self.w[to])

    def first(self, one):
        shift, me = one.shift, self.w["g"]
        p, q = (0, P_ROWS), (P_ROWS, Q_ROWS)
        shift[0].wait_recv()
        self.py = self.along(me, p, "to_y")
        self.pp = [self.along(me, p, "to_xp")]
        self.pm = [self.along(me, p, "to_xm")]
        shift[1].wait_recv()
        self.qp = self.along(me, q, "to_xp")
        self.qm = self.along(me, q, "to_xm")
        self.rest = [self.along(me, q, "to_y")]

    def across(self):
        w = self.w
        self.py.wait_recv()
        p = (0, P_ROWS)
        self.pp.append(self.along(w["yo"] * 4 + w["x"], p, "to_xp"))
        self.pm.append(self.along(w["yo"] * 4 + w["x"], p, "to_xm"))

    def forward_p(self, k):
        w = self.w
        row = (w["yh"], w["yo"])[k] * 4
        self.pp[k].wait_recv()
        self.rest.append(self.along(row + w["xm"], (0, PH), "to_xp"))
        self.pm[k].wait_recv()
        self.rest.append(self.along(row + w["xp"], (PH, PH), "to_xm"))

    def forward_q(self):
        w = self.w
        row, q = w["yh"] * 4, (P_ROWS, Q_ROWS)
        self.qp.wait_recv()
        self.qf = [self.along(row + w["xm"], (P_ROWS, QH), "to_xp")]
        self.rest.append(self.along(row + w["xm"], q, "to_y"))
        self.qm.wait_recv()
        self.qf.append(self.along(row + w["xp"], (P_ROWS + QH, QH), "to_xm"))
        self.rest.append(self.along(row + w["xp"], q, "to_y"))

    def across_q(self):
        w = self.w
        for copy in self.qf:
            copy.wait_recv()
        self.rest.append(self.along(w["yh"] * 4 + w["xo"], (P_ROWS, Q_ROWS), "to_y"))

    def finish(self):
        for copy in self.rest:
            copy.wait_recv()


def chains(keys, count):
    lane = lax.broadcasted_iota(I32, (SLOTS, SLOTS), 1)
    slot = lax.broadcasted_iota(I32, (SLOTS, SLOTS), 0)
    across = jnp.broadcast_to(keys, (SLOTS, SLOTS))
    down = jnp.sum(jnp.where(lane == slot, across, 0), axis=1, keepdims=True)
    live = slot < count

    def latest(where):
        found = jnp.max(jnp.where(where & live, slot, -1), axis=0, keepdims=True)
        return jnp.where(found < 0, SLOTS, found)

    return latest((down == across) & (slot < lane)), latest(down == lane)


def epochs_kernel(
    counts, owner, rows_in, cols_in, ratings, mask_in, users_in, items_in, users_out, items_out,
    rows_v, cols_v, rows_s, cols_s, lists, idx, users, mask, rbuf, err, stage, vown, acc, ub, ubt, vt0, vt1, part,
    r1p, r1m, r2p, r2m, rq, q1p, q1m, q2p, q2m, ry, gsend, grecv, base, total, newv, landing, final,
    rsem, vsem, lsem, send, recv,
):
    w = places()
    copies = Copies(send, recv)
    chunks = SLOTS // GROUP
    stages = stage.shape[0]
    barrier = pltpu.get_barrier_semaphore()
    for peer in PEERS:
        pl.semaphore_signal(barrier, inc=1, device_id=w[peer], device_id_type=MESH)

    def local_copy(src, dst, k):
        copy = pltpu.make_async_copy(src, dst, lsem.at[k])
        copy.start()
        return copy

    lists_in = [
        local_copy(a, b, 3 + k)
        for k, (a, b) in enumerate(((cols_in, cols_v), (rows_in, rows_v), (cols_in, cols_s), (rows_in, rows_s)))
    ]
    users_here = local_copy(users_in, users, 0)

    def items_here(k):
        copy = pltpu.make_async_copy(
            items_in.at[pl.ds(k * OWNERS, OWNERS)], stage.at[k % stages], vsem.at[k]
        )
        copy.start()
        return copy

    arriving = [items_here(k) for k in range(stages)]
    mask_here = local_copy(mask_in, mask, 1)
    own_here = local_copy(items_in.at[pl.ds(w["g"] * OWNERS, OWNERS)], vown, 2)

    def fetch(e, k):
        s = pl.ds(k * GROUP, GROUP)
        return pltpu.make_async_copy(ratings.at[e, s], rbuf.at[s], rsem.at[k])

    def prepare_users(e, first):
        own = jnp.zeros((RANK, RANK), F32)
        for i in range(USER_TILES):
            u = users[pl.ds(i * TILE, TILE), :]
            ub[i] = u.astype(BF16)
            ut = u.T.astype(BF16)
            ubt[0, i], ubt[1, i] = ut[:HALF], ut[HALF:]
            own = own + dot(ut, ub[i])
        own = (own * (GRAM / USER_ROWS) + ridge()).astype(BF16)
        gsend[e, 0] = jnp.where(owner[e] == w["g"], own, jnp.zeros_like(own))
        if first:
            pl.semaphore_wait(barrier, len(PEERS))
        return copies.start(gsend.at[e, 0], grecv.at[e, 0], w["to_y"])

    def spread_gram(e, k, copy):
        copy.wait_recv()
        gsend[e, k] = gsend[e, k - 1] + grecv[e, k - 1]
        return copies.start(gsend.at[e, k], grecv.at[e, k], w["to_x1" if k == 1 else "to_xo"])

    def vtile(vt, j):
        first = j * TILE_UNITS
        return jnp.concatenate(
            [vt[wave, first + u] for wave in range(WAVES) for u in range(TILE_UNITS)], axis=0
        )

    def weights(e, t):
        row = mask[e, pl.ds(t, 1), :].astype(F32)
        return jnp.where(t < counts[e], row, jnp.zeros_like(row))

    def errors(e, vt, t):
        predicted = dot(ub[rows_s[e, t]], vtile(vt, cols_s[e, t]))
        err[t] = (predicted - rbuf[t].astype(F32)).astype(BF16)

    def item_dot(e, wave, t):
        u = ubt[wave, rows_s[e, t]]
        return dot(u * weights(e, t).astype(BF16), err[t])

    def item_add(e, wave, t, add):
        acc[wave, t] = acc[wave, idx[e * LISTS + PREV_COL, t]] + add

    def item_done(e, wave):
        @pl.loop(0, ITEM_TILES, unroll=4)
        def _(j):
            s = pl.ds(pl.multiple_of(lax.rem(j, OWNERS) * HALF, HALF), HALF)
            part[wave, lax.div(j, OWNERS), s, :] = acc[wave, idx[e * LISTS + LAST_COL, j]].astype(BF16)

    def first_pass(e, vt):
        fetch(e, 0).wait()
        for q in range(GROUP):
            errors(e, vt, q)

        @pl.loop(0, chunks - 1)
        def _(g):
            adds = [item_dot(e, 0, g * GROUP + q) for q in range(GROUP)]
            fetch(e, g + 1).wait()
            for q in range(GROUP):
                errors(e, vt, (g + 1) * GROUP + q)
            for q in range(GROUP):
                item_add(e, 0, g * GROUP + q, adds[q])

        adds = [item_dot(e, 0, SLOTS - GROUP + q) for q in range(GROUP)]
        for q in range(GROUP):
            item_add(e, 0, SLOTS - GROUP + q, adds[q])
        item_done(e, 0)

    def second_pass(e):
        @pl.loop(0, chunks)
        def _(g):
            adds = [item_dot(e, 1, g * GROUP + q) for q in range(GROUP)]
            for q in range(GROUP):
                item_add(e, 1, g * GROUP + q, adds[q])

        item_done(e, 1)

    def user_pass(e, vt, first, last):
        @pl.loop(first, last)
        def _(g):
            def add_dot(t):
                return dot(vtile(vt, cols_s[e, t]), err[t], 1, 1) * weights(e, t)

            for h in range(2):
                slots = [g * GROUP + h * (GROUP // 2) + q for q in range(GROUP // 2)]
                adds = [add_dot(t) for t in slots]
                for t, add in zip(slots, adds):
                    before = idx[e * LISTS + PREV_ROW, t]
                    acc[0, t] = acc[0, before] + add[:HALF]
                    acc[1, t] = acc[1, before] + add[HALF:]

    def item_gram(vt):
        def add(j, gram):
            for q in range(4):
                v = vtile(vt, j * 4 + q)
                gram = gram + dot(v, v, 1, 1)
            return gram

        gram = lax.fori_loop(0, ITEM_TILES // 4, add, jnp.zeros((RANK, RANK), F32))
        return gram * (GRAM / (ITEM_TILES * TILE)) + ridge()

    def user_update(e, pull):
        @pl.loop(0, USER_TILES)
        def _(i):
            s = pl.ds(pl.multiple_of(i * TILE, TILE), TILE)
            u = users[s, :]
            at = idx[e * LISTS + LAST_ROW, i]
            grad = jnp.concatenate([acc[0, at], acc[1, at]], axis=0)
            users[s, :] = u - LEARN * (grad.T + dot(u, pull, precision=HIGHEST))

    def item_base(e, copy):
        copy.wait_recv()
        pull = (gsend[e, 2] + grecv[e, 2]).astype(F32)

        @pl.loop(0, OWNERS)
        def _(k):
            if e == 0:
                v = vown[k].T
            else:
                v = vtile(vt1, w["g"] * OWNERS + k).astype(F32)
            base[k] = v - LEARN * dot(pull, v, 0, 0, precision=HIGHEST)

    bufs = dict(
        r1p=r1p, r1m=r1m, r2p=r2p, r2m=r2m, rq=rq, q1p=q1p, q1m=q1m, q2p=q2p, q2m=q2m, ry=ry
    )

    def sums(e):
        at = {k: v.at[e] for k, v in bufs.items()}
        return [Sum(copies, w, wave, part, at, base, total, newv) for wave in range(WAVES)]

    for copy in lists_in:
        copy.wait()
    for e in range(ratings.shape[0]):
        for k, keys in enumerate((cols_v, rows_v)):
            prev, final_slot = chains(keys[e : e + 1, :], counts[e])
            at = e * LISTS + k
            lists[at : at + 1, 0:SLOTS] = prev
            lists[at + 2 : at + 3, 0:SLOTS] = final_slot
    lists_out = local_copy(lists, idx, 7)
    users_here.wait()
    gram_copy = prepare_users(0, True)
    zero = jnp.zeros((HALF, TILE), F32)
    acc[0, SLOTS] = zero
    acc[1, SLOTS] = zero
    for k in range(OWNERS):
        arriving[k].wait()

        @pl.loop(0, OWNERS, unroll=2)
        def _(j):
            v = stage[k % stages, j].T.astype(BF16)
            for u in range(TILE_UNITS):
                at = (k * OWNERS + j) * TILE_UNITS + u
                vt0[0, at] = v[u * UNIT : (u + 1) * UNIT]
                vt0[1, at] = v[HALF + u * UNIT : HALF + (u + 1) * UNIT]

        if k + stages < OWNERS:
            arriving.append(items_here(k + stages))
        for c in range(chunks // OWNERS * k, chunks // OWNERS * (k + 1)):
            fetch(0, c).start()
    gram_copy = spread_gram(0, 1, gram_copy)
    mask_here.wait()
    lists_out.wait()
    own_here.wait()

    def steps(e, vt, landing, gather):
        waves = sums(e)
        table = {}
        for k, one in enumerate(waves):
            table.update({
                "s%d" % k: one.start, "p%d" % k: one.pass_p, "f%d" % k: one.far_q, "n%d" % k: one.near_q,
                "q%d" % k: one.pass_q, "c%d" % k: one.cross_p,
                "F%d" % k: functools.partial(one.finish, landing),
            })
            if gather is not None:
                to = Gather(copies, w, k, gather)
                table.update({
                    "a%d" % k: functools.partial(to.first, one), "x%d" % k: to.across,
                    "k%d" % k: functools.partial(to.forward_p, 0), "r%d" % k: to.forward_q,
                    "l%d" % k: functools.partial(to.forward_p, 1), "z%d" % k: to.across_q, "e%d" % k: to.finish,
                })
        done = [0]

        def some_users():
            user_pass(e, vt, done[0], done[0] + 2)
            done[0] += 2

        table.update(B=functools.partial(second_pass, e), U=some_users)
        table["V"] = lambda: user_update(e, item_gram(vt))
        return waves, table

    first_pass(0, vt0)
    gram_copy = spread_gram(0, 2, gram_copy)
    waves, table = steps(0, vt0, (vt1, w["g"]), vt1)
    table["I"] = lambda: item_base(0, gram_copy)
    for k in range(chunks):
        fetch(1, k).start()
    for step in ORDER_0:
        table[step]()
    gram_copy = prepare_users(1, False)
    table["e0"]()
    gram_copy = spread_gram(1, 1, gram_copy)
    table["e1"]()
    copies.finish()

    first_pass(1, vt1)
    gram_copy = spread_gram(1, 2, gram_copy)
    waves, table = steps(1, vt1, (landing, 0), None)
    table["I"] = lambda: item_base(1, gram_copy)
    sent = []
    table["O"] = lambda: sent.append(local_copy(users, users_out, 0))
    for step in ORDER_1:
        table[step]()
    users_gone = sent[0]
    s0, s1 = waves
    for copy in s0.shift + s1.shift:
        copy.wait_recv()

    @pl.loop(0, OWNERS)
    def _(k):
        v = vtile(landing, k).astype(F32)
        final[pl.ds(pl.multiple_of(k * TILE, TILE), TILE), :] = v.T

    items_gone = local_copy(final, items_out, 1)
    copies.finish()
    users_gone.wait()
    items_gone.wait()


def epochs(counts, owner, rows, cols, ratings, mask, users, items):
    smem = pl.BlockSpec(memory_space=pltpu.SMEM)
    anywhere = pl.BlockSpec(memory_space=pl.ANY)
    dma = pltpu.SemaphoreType.DMA
    count = ratings.shape[0]

    def wide(*rows):
        return pltpu.VMEM((count, WAVES, *rows, TILE), BF16)

    return pl.pallas_call(
        epochs_kernel,
        out_shape=[jax.ShapeDtypeStruct(users.shape, F32), jax.ShapeDtypeStruct(users.shape, F32)],
        in_specs=[smem] * 2 + [anywhere] * 6,
        out_specs=[anywhere, anywhere],
        scratch_shapes=[
            pltpu.VMEM(rows.shape, I32),
            pltpu.VMEM(cols.shape, I32),
            pltpu.SMEM(rows.shape, I32),
            pltpu.SMEM(cols.shape, I32),
            pltpu.VMEM((count * LISTS, 128), I32),
            pltpu.SMEM((count * LISTS, 128), I32),
            pltpu.VMEM(users.shape, F32),
            pltpu.VMEM(mask.shape, I32),
            pltpu.VMEM((SLOTS, TILE, TILE), BF16),
            pltpu.VMEM((SLOTS, TILE, TILE), BF16),
            pltpu.VMEM((4, OWNERS, TILE, RANK), F32),
            pltpu.VMEM((OWNERS, TILE, RANK), F32),
            pltpu.VMEM((WAVES, SLOTS + 1, HALF, TILE), F32),
            pltpu.VMEM((USER_TILES, TILE, RANK), BF16),
            pltpu.VMEM((WAVES, USER_TILES, HALF, TILE), BF16),
            pltpu.VMEM((WAVES, OWNERS * WAVE_UNITS, UNIT, TILE), BF16),
            pltpu.VMEM((WAVES, OWNERS * WAVE_UNITS, UNIT, TILE), BF16),
            pltpu.VMEM((WAVES, OWNERS, WAVE_ROWS, TILE), BF16),
            wide(2, PH), wide(2, PH), wide(2, P_ROWS), wide(2, P_ROWS),
            wide(4, Q_ROWS), wide(QH), wide(QH), wide(Q_ROWS), wide(Q_ROWS), wide(P_ROWS),
            pltpu.VMEM((count, 3, RANK, RANK), BF16),
            pltpu.VMEM((count, 3, RANK, RANK), BF16),
            pltpu.VMEM((OWNERS, RANK, TILE), F32),
            pltpu.VMEM((WAVES, WAVE_ROWS, TILE), F32),
            pltpu.VMEM((WAVES, WAVE_UNITS, UNIT, TILE), BF16),
            pltpu.VMEM((WAVES, WAVE_UNITS, UNIT, TILE), BF16),
            pltpu.VMEM(users.shape, F32),
            dma((SLOTS // GROUP,)),
            dma((OWNERS,)),
            dma((8,)),
            dma((COPIES,)),
            dma((COPIES,)),
        ],
        compiler_params=pltpu.CompilerParams(
            collective_id=0, has_side_effects=True, vmem_limit_bytes=62 * 2**20
        ),
        name="epochs",
    )(counts, owner, rows, cols, ratings, mask, users, items)


PIECES = 4


def settle_kernel(a, b, a_out, b_out, a_here, b_here, come, go):
    rows = a.shape[0] // PIECES
    moves = []
    for src, here, dst in ((a, a_here, a_out), (b, b_here, b_out)):
        for k in range(PIECES):
            s, n = pl.ds(k * rows, rows), len(moves)
            moves.append(
                (
                    pltpu.make_async_copy(src.at[s], here.at[s], come.at[n]),
                    pltpu.make_async_copy(here.at[s], dst.at[s], go.at[n]),
                )
            )
    for first, _ in moves:
        first.start()
    for first, second in moves:
        first.wait()
        second.start()
    for _, second in moves:
        second.wait()


def settled(a, b):
    anywhere = pl.BlockSpec(memory_space=pl.ANY)
    dma = pltpu.SemaphoreType.DMA
    return pl.pallas_call(
        settle_kernel,
        out_shape=[jax.ShapeDtypeStruct(a.shape, a.dtype), jax.ShapeDtypeStruct(b.shape, b.dtype)],
        in_specs=[anywhere] * 2,
        out_specs=[anywhere] * 2,
        scratch_shapes=[
            pltpu.VMEM(a.shape, a.dtype),
            pltpu.VMEM(b.shape, b.dtype),
            dma((2 * PIECES,)),
            dma((2 * PIECES,)),
        ],
        name="settle",
    )(a, b)


def local(ratings, row_index, col_index, row_mask, counts, owner_list, user_factors, item_factors):
    count = ratings.shape[0]
    users, items = epochs(
        counts.reshape(count),
        owner_list.reshape(count),
        row_index.reshape(count, SLOTS),
        col_index.reshape(count, SLOTS),
        ratings.reshape(count, SLOTS, TILE, TILE),
        row_mask.reshape(count, SLOTS, TILE),
        user_factors,
        item_factors.reshape(ITEM_TILES, TILE, RANK),
    )
    return settled(users, items)


def solution(mesh):
    in_specs = (
        P(None, "blk", "grp", None, None, None),
        P(None, "blk", "grp", None),
        P(None, "blk", "grp", None),
        P(None, "blk", "grp", None, None),
        P(None, "blk", "grp"),
        P(None, "blk"),
        P(("blk", "grp"), None),
        P("blk", None),
    )
    out_specs = (P(("blk", "grp"), None), P(("blk", "grp"), None))
    return jax.shard_map(local, mesh=mesh, in_specs=in_specs, out_specs=out_specs, check_vma=False)
```

```python
import functools

import jax
import jax.numpy as jnp
from jax import lax
from jax.experimental import pallas as pl
from jax.experimental.pallas import tpu as pltpu
from jax.sharding import PartitionSpec as P

LEARN = 0.004
GRAM = 256.0
RIDGE = 1.0

TILE = 256
RANK = 128
SLOTS = 64
USER_TILES = 8
ITEM_TILES = 64
OWNERS = 8
GROUP = 8
USER_ROWS = USER_TILES * TILE

WAVES = 2
HALF = RANK // WAVES
WAVE_ROWS = 8 * HALF
P_ROWS = 288
Q_ROWS = WAVE_ROWS - P_ROWS
PH, QH = P_ROWS // 2, Q_ROWS // 2
UNIT = 16
TILE_UNITS = HALF // UNIT
WAVE_UNITS = WAVE_ROWS // UNIT


def units(owner, start, rows):
    return pl.ds(owner * WAVE_UNITS + start // UNIT, rows // UNIT)


PREV_COL, PREV_ROW, LAST_COL, LAST_ROW, LISTS = 0, 1, 2, 3, 4

F32, BF16, I32 = jnp.float32, jnp.bfloat16, jnp.int32
MESH = pl.DeviceIdType.MESH
HIGHEST = lax.Precision.HIGHEST


def dot(a, b, ca=1, cb=0, precision=None):
    return lax.dot_general(
        a, b, (((ca,), (cb,)), ((), ())), precision=precision, preferred_element_type=F32
    )


def ridge():
    row = lax.broadcasted_iota(I32, (RANK, RANK), 0)
    col = lax.broadcasted_iota(I32, (RANK, RANK), 1)
    return jnp.where(row == col, RIDGE, 0.0).astype(F32)


def places():
    b, g = lax.axis_index("blk"), lax.axis_index("grp")
    blocks = lax.axis_size("blk")
    x, yh = g % 4, g // 4
    xp, xm, xo, yo = (x + 1) % 4, (x + 3) % 4, (x + 2) % 4, 1 - yh
    x1 = x + 1 - 2 * (x % 2)
    return dict(
        b=b, g=g, x=x, yh=yh, xp=xp, xm=xm, xo=xo, yo=yo,
        to_xp=(b, yh * 4 + xp), to_xm=(b, yh * 4 + xm), to_xo=(b, yh * 4 + xo),
        to_x1=(b, yh * 4 + x1), to_y=(b, yo * 4 + x),
        to_next=((b + 1) % blocks, g), to_last=((b + blocks - 1) % blocks, g),
    )


PEERS = ("to_xp", "to_xm", "to_xo", "to_y", "to_next", "to_last")


def in_steps(count, step, fn):
    if count == step:
        fn(0)
        return

    @pl.loop(0, count // step)
    def _(k):
        fn(pl.multiple_of(k * step, step))


class Copies:
    def __init__(self, send, recv):
        self.send, self.recv, self.used, self.open = send, recv, 0, []

    def start(self, src, dst, to):
        k = self.used
        assert k < COPIES
        self.used += 1
        copy = pltpu.make_async_remote_copy(
            src_ref=src, dst_ref=dst, send_sem=self.send.at[k], recv_sem=self.recv.at[k],
            device_id=to, device_id_type=MESH,
        )
        copy.start()
        self.open.append(copy)
        return copy

    def finish(self):
        for copy in self.open:
            copy.wait_send()
        self.open = []


COPIES = 160

ORDER_0 = (
    "s0", "g0", "t0", "B", "U", "p0", "s1", "c0", "P0", "v0", "U", "f0", "u0", "g1", "I", "n0",
    "p1", "q0", "u1", "t1", "v1", "C0", "F0", "f1", "P1", "c1", "n1", "q1", "a0", "U", "b0", "C1",
    "F1", "x0", "U", "a1", "r0", "b1", "x1", "z0", "V", "l0", "r1", "l1", "z1", "k0", "k1",
)
ORDER_1 = (
    "s0", "g0", "B", "s1", "p0", "t0", "g1", "u0", "P0", "f0", "u1", "U", "t1", "U", "I", "c0",
    "v1", "v0", "U", "n0", "p1", "U", "f1", "q0", "n1", "P1", "c1", "C0", "q1", "F0", "C1", "F1",
    "V", "O",
)


class Sum:
    def __init__(self, copies, w, wave, part, bufs, base, total, newv):
        self.c, self.w, self.wave = copies, w, wave
        self.part = part.at[wave]
        self.bufs = {k: v.at[wave] for k, v in bufs.items()}
        self.base, self.total, self.newv = base, total.at[wave], newv.at[wave]

    def start(self):
        w, c, part, b, xo = self.w, self.c, self.part, self.bufs, self.w["xo"]
        self.rows = (w["yo"], w["yh"])
        self.one_p, self.one_m, self.q, self.two = [], [], {}, [[], []]
        for a in self.rows:
            self.one_p.append(c.start(part.at[a * 4 + xo, pl.ds(0, PH)], b["r1p"].at[a], w["to_xp"]))
            self.one_m.append(c.start(part.at[a * 4 + xo, pl.ds(PH, PH)], b["r1m"].at[a], w["to_xm"]))
        self.send_q("xo")

    def send_q(self, *names):
        w = self.w
        for name in names:
            self.q[name] = self.c.start(
                self.part.at[w["yo"] * 4 + w[name], pl.ds(P_ROWS, Q_ROWS)], self.bufs["rq"].at[w[name]], w["to_y"]
            )

    def send_p(self, k):
        w, c, part, b, a = self.w, self.c, self.part, self.bufs, self.rows[k]
        pa, pb = pl.ds(0, PH), pl.ds(PH, PH)
        self.two[k].append(c.start(part.at[a * 4 + w["xp"], pb], b["r2p"].at[a, pb], w["to_xp"]))
        self.two[k].append(c.start(part.at[a * 4 + w["xm"], pa], b["r2m"].at[a, pa], w["to_xm"]))

    def pass_p(self, k):
        w, c, part, b, a = self.w, self.c, self.part, self.bufs, self.rows[k]
        xp, xm = w["xp"], w["xm"]
        self.one_p[k].wait_recv()

        def fn(at):
            s = pl.ds(at, 48)
            both = b["r1p"][a, s, :].astype(F32) + part[a * 4 + xp, s, :].astype(F32)
            b["r1p"][a, s, :] = both.astype(BF16)

        in_steps(PH, 48, fn)
        self.two[k].append(c.start(b["r1p"].at[a], b["r2p"].at[a, pl.ds(0, PH)], w["to_xp"]))
        self.one_m[k].wait_recv()

        def fn(at):
            s, t = pl.ds(at, 48), pl.ds(at + PH, 48)
            both = b["r1m"][a, s, :].astype(F32) + part[a * 4 + xm, t, :].astype(F32)
            b["r1m"][a, s, :] = both.astype(BF16)

        in_steps(PH, 48, fn)
        self.two[k].append(c.start(b["r1m"].at[a], b["r2m"].at[a, pl.ds(PH, PH)], w["to_xm"]))

    def add_q(self, copy, d):
        part, b, yh = self.part, self.bufs, self.w["yh"]
        copy.wait_recv()

        def fn(k):
            s, t = pl.ds(k, 112), pl.ds(k + P_ROWS, 112)
            both = b["rq"][d, s, :].astype(F32) + part[yh * 4 + d, t, :].astype(F32)
            b["rq"][d, s, :] = both.astype(BF16)

        in_steps(Q_ROWS, 112, fn)

    def far_q(self):
        w, c, b, xo = self.w, self.c, self.bufs, self.w["xo"]
        self.add_q(self.q["xo"], xo)
        self.q1p = c.start(b["rq"].at[xo, pl.ds(0, QH)], b["q1p"], w["to_xp"])
        self.q1m = c.start(b["rq"].at[xo, pl.ds(QH, QH)], b["q1m"], w["to_xm"])

    def near_q(self):
        w, c, b, xp, xm = self.w, self.c, self.bufs, self.w["xp"], self.w["xm"]
        qa, qb = pl.ds(0, QH), pl.ds(QH, QH)
        self.add_q(self.q["xp"], xp)
        self.q2 = [c.start(b["rq"].at[xp, qb], b["q2p"].at[qb], w["to_xp"])]
        self.add_q(self.q["xm"], xm)
        self.q2.append(c.start(b["rq"].at[xm, qa], b["q2m"].at[qa], w["to_xm"]))

    def pass_q(self):
        w, c, b, xp, xm = self.w, self.c, self.bufs, self.w["xp"], self.w["xm"]
        self.q1p.wait_recv()
        b["q1p"][...] = (b["q1p"][...].astype(F32) + b["rq"][xp, pl.ds(0, QH), :].astype(F32)).astype(BF16)
        self.q2.append(c.start(b["q1p"], b["q2p"].at[pl.ds(0, QH)], w["to_xp"]))
        self.q1m.wait_recv()
        b["q1m"][...] = (b["q1m"][...].astype(F32) + b["rq"][xm, pl.ds(QH, QH), :].astype(F32)).astype(BF16)
        self.q2.append(c.start(b["q1m"], b["q2m"].at[pl.ds(QH, QH)], w["to_xm"]))

    def sum_p(self, a, s):
        part, b = self.part, self.bufs
        both = b["r2p"][a, s, :].astype(F32) + b["r2m"][a, s, :].astype(F32)
        return both + part[a * 4 + self.w["x"], s, :].astype(F32)

    def cross_p(self):
        w, b, yo = self.w, self.bufs, self.w["yo"]
        for copy in self.two[0]:
            copy.wait_recv()

        def fn(k):
            s = pl.ds(k, 48)
            b["r2p"][yo, s, :] = self.sum_p(yo, s).astype(BF16)

        in_steps(P_ROWS, 48, fn)
        self.y = self.c.start(b["r2p"].at[yo], b["ry"], w["to_y"])

    def keep_p(self):
        yh = self.w["yh"]
        for copy in self.two[1]:
            copy.wait_recv()

        def fn(k):
            s = pl.ds(k, 48)
            self.total[s, :] = self.sum_p(yh, s)

        in_steps(P_ROWS, 48, fn)

    def finish(self, landing):
        w, b, x, total = self.w, self.bufs, self.w["x"], self.total
        self.add_q(self.q["x"], x)
        for copy in self.q2:
            copy.wait_recv()

        def fn(k):
            s, t = pl.ds(k, 112), pl.ds(k + P_ROWS, 112)
            both = b["q2p"][s, :].astype(F32) + b["q2m"][s, :].astype(F32)
            total[t, :] = b["rq"][x, s, :].astype(F32) + both

        in_steps(Q_ROWS, 112, fn)
        self.y.wait_recv()

        def fn(k):
            s = pl.ds(k, 48)
            total[s, :] = total[s, :] + b["ry"][s, :].astype(F32)

        in_steps(P_ROWS, 48, fn)

        @pl.loop(0, OWNERS)
        def _(k):
            s = pl.ds(pl.multiple_of(k * HALF, HALF), HALF)
            old = self.base[k, pl.ds(HALF * self.wave, HALF), :]
            new = (old - LEARN * total[s, :]).astype(BF16)
            for u in range(TILE_UNITS):
                self.newv[k * TILE_UNITS + u] = new[u * UNIT : (u + 1) * UNIT]

        landing, owner = landing
        landing = landing.at[self.wave]
        self.shift = [
            self.c.start(self.newv.at[units(0, at, n)], landing.at[units(owner, at, n)], w["to_next"])
            for at, n in ((0, P_ROWS), (P_ROWS, Q_ROWS))
        ]


class Gather:
    def __init__(self, copies, w, wave, vt):
        self.c, self.w, self.vt = copies, w, vt.at[wave]

    def along(self, owner, rows, to):
        ref = self.vt.at[units(owner, *rows)]
        return self.c.start(ref, ref, self.w[to])

    def first(self, one):
        shift, me = one.shift, self.w["g"]
        p = (0, P_ROWS)
        shift[0].wait_recv()
        self.py = self.along(me, p, "to_y")
        self.pp = [self.along(me, p, "to_xp")]
        self.pm = [self.along(me, p, "to_xm")]

    def first_q(self, one):
        me, q = self.w["g"], (P_ROWS, Q_ROWS)
        one.shift[1].wait_recv()
        self.qp = self.along(me, q, "to_xp")
        self.qm = self.along(me, q, "to_xm")
        self.rest = [self.along(me, q, "to_y")]

    def across(self):
        w = self.w
        self.py.wait_recv()
        p = (0, P_ROWS)
        self.pp.append(self.along(w["yo"] * 4 + w["x"], p, "to_xp"))
        self.pm.append(self.along(w["yo"] * 4 + w["x"], p, "to_xm"))

    def forward_p(self, k):
        w = self.w
        row = (w["yh"], w["yo"])[k] * 4
        self.pp[k].wait_recv()
        self.rest.append(self.along(row + w["xm"], (0, PH), "to_xp"))
        self.pm[k].wait_recv()
        self.rest.append(self.along(row + w["xp"], (PH, PH), "to_xm"))

    def forward_q(self):
        w = self.w
        row, q = w["yh"] * 4, (P_ROWS, Q_ROWS)
        self.qp.wait_recv()
        self.qf = [self.along(row + w["xm"], (P_ROWS, QH), "to_xp")]
        self.rest.append(self.along(row + w["xm"], q, "to_y"))
        self.qm.wait_recv()
        self.qf.append(self.along(row + w["xp"], (P_ROWS + QH, QH), "to_xm"))
        self.rest.append(self.along(row + w["xp"], q, "to_y"))

    def across_q(self):
        w = self.w
        for copy in self.qf:
            copy.wait_recv()
        self.rest.append(self.along(w["yh"] * 4 + w["xo"], (P_ROWS, Q_ROWS), "to_y"))

    def finish(self):
        for copy in self.rest:
            copy.wait_recv()


def chains(keys, count):
    lane = lax.broadcasted_iota(I32, (SLOTS, SLOTS), 1)
    slot = lax.broadcasted_iota(I32, (SLOTS, SLOTS), 0)
    across = jnp.broadcast_to(keys, (SLOTS, SLOTS))
    down = jnp.sum(jnp.where(lane == slot, across, 0), axis=1, keepdims=True)
    live = slot < count

    def latest(where):
        found = jnp.max(jnp.where(where & live, slot, -1), axis=0, keepdims=True)
        return jnp.where(found < 0, SLOTS, found)

    return latest((down == across) & (slot < lane)), latest(down == lane)


def epochs_kernel(
    counts, owner, rows_in, cols_in, ratings, mask_in, users_in, items_in, users_out, items_out,
    rows_v, cols_v, rows_s, cols_s, lists, idx, users, mask, rbuf, err, stage, vown, acc, ub, ubt, vt0, vt1, part,
    r1p, r1m, r2p, r2m, rq, q1p, q1m, q2p, q2m, ry, gsend, grecv, base, total, newv, landing, final,
    rsem, vsem, lsem, send, recv,
):
    w = places()
    copies = Copies(send, recv)
    chunks = SLOTS // GROUP
    stages = stage.shape[0]
    barrier = pltpu.get_barrier_semaphore()
    for peer in PEERS:
        pl.semaphore_signal(barrier, inc=1, device_id=w[peer], device_id_type=MESH)

    def local_copy(src, dst, k):
        copy = pltpu.make_async_copy(src, dst, lsem.at[k])
        copy.start()
        return copy

    lists_in = [
        local_copy(a, b, 3 + k)
        for k, (a, b) in enumerate(((cols_in, cols_v), (rows_in, rows_v), (cols_in, cols_s), (rows_in, rows_s)))
    ]
    users_here = local_copy(users_in, users, 0)

    def items_here(k):
        copy = pltpu.make_async_copy(
            items_in.at[pl.ds(k * OWNERS, OWNERS)], stage.at[k % stages], vsem.at[k]
        )
        copy.start()
        return copy

    arriving = [items_here(k) for k in range(stages)]
    mask_here = local_copy(mask_in, mask, 1)
    own_here = local_copy(items_in.at[pl.ds(w["g"] * OWNERS, OWNERS)], vown, 2)

    def fetch(e, k):
        s = pl.ds(k * GROUP, GROUP)
        return pltpu.make_async_copy(ratings.at[e, s], rbuf.at[s], rsem.at[k])

    def prepare_users(e, first):
        own = jnp.zeros((RANK, RANK), F32)
        for i in range(USER_TILES):
            u = users[pl.ds(i * TILE, TILE), :]
            ub[i] = u.astype(BF16)
            ut = u.T.astype(BF16)
            ubt[0, i], ubt[1, i] = ut[:HALF], ut[HALF:]
            own = own + dot(ut, ub[i])
        own = (own * (GRAM / USER_ROWS) + ridge()).astype(BF16)
        gsend[e, 0] = jnp.where(owner[e] == w["g"], own, jnp.zeros_like(own))
        if first:
            pl.semaphore_wait(barrier, len(PEERS))
        return copies.start(gsend.at[e, 0], grecv.at[e, 0], w["to_y"])

    def spread_gram(e, k, copy):
        copy.wait_recv()
        gsend[e, k] = gsend[e, k - 1] + grecv[e, k - 1]
        return copies.start(gsend.at[e, k], grecv.at[e, k], w["to_x1" if k == 1 else "to_xo"])

    def vtile(vt, j):
        first = j * TILE_UNITS
        return jnp.concatenate(
            [vt[wave, first + u] for wave in range(WAVES) for u in range(TILE_UNITS)], axis=0
        )

    def weights(e, t):
        row = mask[e, pl.ds(t, 1), :].astype(F32)
        return jnp.where(t < counts[e], row, jnp.zeros_like(row))

    def errors(e, vt, t):
        predicted = dot(ub[rows_s[e, t]], vtile(vt, cols_s[e, t]))
        err[t] = (predicted - rbuf[t].astype(F32)).astype(BF16)

    def item_dot(e, wave, t):
        u = ubt[wave, rows_s[e, t]]
        return dot(u * weights(e, t).astype(BF16), err[t])

    def item_add(e, wave, t, add):
        acc[wave, t] = acc[wave, idx[e * LISTS + PREV_COL, t]] + add

    def item_done(e, wave):
        @pl.loop(0, ITEM_TILES, unroll=4)
        def _(j):
            s = pl.ds(pl.multiple_of(lax.rem(j, OWNERS) * HALF, HALF), HALF)
            part[wave, lax.div(j, OWNERS), s, :] = acc[wave, idx[e * LISTS + LAST_COL, j]].astype(BF16)

    def first_pass(e, vt):
        fetch(e, 0).wait()
        for q in range(GROUP):
            errors(e, vt, q)

        @pl.loop(0, chunks - 1)
        def _(g):
            adds = [item_dot(e, 0, g * GROUP + q) for q in range(GROUP)]
            fetch(e, g + 1).wait()
            for q in range(GROUP):
                errors(e, vt, (g + 1) * GROUP + q)
            for q in range(GROUP):
                item_add(e, 0, g * GROUP + q, adds[q])

        adds = [item_dot(e, 0, SLOTS - GROUP + q) for q in range(GROUP)]
        for q in range(GROUP):
            item_add(e, 0, SLOTS - GROUP + q, adds[q])
        item_done(e, 0)

    def second_pass(e):
        @pl.loop(0, chunks)
        def _(g):
            adds = [item_dot(e, 1, g * GROUP + q) for q in range(GROUP)]
            for q in range(GROUP):
                item_add(e, 1, g * GROUP + q, adds[q])

        item_done(e, 1)

    def user_pass(e, vt, first, last):
        @pl.loop(first, last)
        def _(g):
            def add_dot(t):
                return dot(vtile(vt, cols_s[e, t]), err[t], 1, 1) * weights(e, t)

            for h in range(2):
                slots = [g * GROUP + h * (GROUP // 2) + q for q in range(GROUP // 2)]
                adds = [add_dot(t) for t in slots]
                for t, add in zip(slots, adds):
                    before = idx[e * LISTS + PREV_ROW, t]
                    acc[0, t] = acc[0, before] + add[:HALF]
                    acc[1, t] = acc[1, before] + add[HALF:]

    def item_gram(vt):
        def add(j, gram):
            for q in range(4):
                v = vtile(vt, j * 4 + q)
                gram = gram + dot(v, v, 1, 1)
            return gram

        gram = lax.fori_loop(0, ITEM_TILES // 4, add, jnp.zeros((RANK, RANK), F32))
        return gram * (GRAM / (ITEM_TILES * TILE)) + ridge()

    def user_update(e, pull):
        @pl.loop(0, USER_TILES)
        def _(i):
            s = pl.ds(pl.multiple_of(i * TILE, TILE), TILE)
            u = users[s, :]
            at = idx[e * LISTS + LAST_ROW, i]
            grad = jnp.concatenate([acc[0, at], acc[1, at]], axis=0)
            users[s, :] = u - LEARN * (grad.T + dot(u, pull, precision=HIGHEST))

    def item_base(e, copy):
        copy.wait_recv()
        pull = (gsend[e, 2] + grecv[e, 2]).astype(F32)

        @pl.loop(0, OWNERS)
        def _(k):
            if e == 0:
                v = vown[k].T
            else:
                v = vtile(vt1, w["g"] * OWNERS + k).astype(F32)
            base[k] = v - LEARN * dot(pull, v, 0, 0, precision=HIGHEST)

    bufs = dict(
        r1p=r1p, r1m=r1m, r2p=r2p, r2m=r2m, rq=rq, q1p=q1p, q1m=q1m, q2p=q2p, q2m=q2m, ry=ry
    )

    def sums(e):
        at = {k: v.at[e] for k, v in bufs.items()}
        return [Sum(copies, w, wave, part, at, base, total, newv) for wave in range(WAVES)]

    for copy in lists_in:
        copy.wait()
    for e in range(ratings.shape[0]):
        for k, keys in enumerate((cols_v, rows_v)):
            prev, final_slot = chains(keys[e : e + 1, :], counts[e])
            at = e * LISTS + k
            lists[at : at + 1, 0:SLOTS] = prev
            lists[at + 2 : at + 3, 0:SLOTS] = final_slot
    lists_out = local_copy(lists, idx, 7)
    users_here.wait()
    gram_copy = prepare_users(0, True)
    zero = jnp.zeros((HALF, TILE), F32)
    acc[0, SLOTS] = zero
    acc[1, SLOTS] = zero
    for k in range(OWNERS):
        arriving[k].wait()

        @pl.loop(0, OWNERS, unroll=2)
        def _(j):
            v = stage[k % stages, j].T.astype(BF16)
            for u in range(TILE_UNITS):
                at = (k * OWNERS + j) * TILE_UNITS + u
                vt0[0, at] = v[u * UNIT : (u + 1) * UNIT]
                vt0[1, at] = v[HALF + u * UNIT : HALF + (u + 1) * UNIT]

        if k + stages < OWNERS:
            arriving.append(items_here(k + stages))
        for c in range(chunks // OWNERS * k, chunks // OWNERS * (k + 1)):
            fetch(0, c).start()
    gram_copy = spread_gram(0, 1, gram_copy)
    mask_here.wait()
    lists_out.wait()
    own_here.wait()

    def steps(e, vt, landing, gather):
        waves = sums(e)
        table = {}
        for k, one in enumerate(waves):
            table.update({
                "s%d" % k: one.start, "g%d" % k: functools.partial(one.send_q, "xp", "xm"),
                "u%d" % k: functools.partial(one.send_q, "x"), "t%d" % k: functools.partial(one.send_p, 0),
                "v%d" % k: functools.partial(one.send_p, 1), "p%d" % k: functools.partial(one.pass_p, 0),
                "P%d" % k: functools.partial(one.pass_p, 1), "f%d" % k: one.far_q, "n%d" % k: one.near_q,
                "q%d" % k: one.pass_q, "c%d" % k: one.cross_p, "C%d" % k: one.keep_p,
                "F%d" % k: functools.partial(one.finish, landing),
            })
            if gather is not None:
                to = Gather(copies, w, k, gather)
                table.update({
                    "a%d" % k: functools.partial(to.first, one), "b%d" % k: functools.partial(to.first_q, one), "x%d" % k: to.across,
                    "k%d" % k: functools.partial(to.forward_p, 0), "r%d" % k: to.forward_q,
                    "l%d" % k: functools.partial(to.forward_p, 1), "z%d" % k: to.across_q, "e%d" % k: to.finish,
                })
        done = [0]

        def some_users():
            user_pass(e, vt, done[0], done[0] + 2)
            done[0] += 2

        table.update(B=functools.partial(second_pass, e), U=some_users)
        table["V"] = lambda: user_update(e, item_gram(vt))
        return waves, table

    first_pass(0, vt0)
    gram_copy = spread_gram(0, 2, gram_copy)
    waves, table = steps(0, vt0, (vt1, w["g"]), vt1)
    table["I"] = lambda: item_base(0, gram_copy)
    for k in range(chunks):
        fetch(1, k).start()
    for step in ORDER_0:
        table[step]()
    gram_copy = prepare_users(1, False)
    table["e0"]()
    gram_copy = spread_gram(1, 1, gram_copy)
    table["e1"]()
    copies.finish()

    first_pass(1, vt1)
    gram_copy = spread_gram(1, 2, gram_copy)
    waves, table = steps(1, vt1, (landing, 0), None)
    table["I"] = lambda: item_base(1, gram_copy)
    sent = []
    table["O"] = lambda: sent.append(local_copy(users, users_out, 0))
    for step in ORDER_1:
        table[step]()
    users_gone = sent[0]
    s0, s1 = waves
    for copy in s0.shift + s1.shift:
        copy.wait_recv()

    @pl.loop(0, OWNERS)
    def _(k):
        v = vtile(landing, k).astype(F32)
        final[pl.ds(pl.multiple_of(k * TILE, TILE), TILE), :] = v.T

    items_gone = local_copy(final, items_out, 1)
    copies.finish()
    users_gone.wait()
    items_gone.wait()


def epochs(counts, owner, rows, cols, ratings, mask, users, items):
    smem = pl.BlockSpec(memory_space=pltpu.SMEM)
    anywhere = pl.BlockSpec(memory_space=pl.ANY)
    dma = pltpu.SemaphoreType.DMA
    count = ratings.shape[0]

    def wide(*rows):
        return pltpu.VMEM((count, WAVES, *rows, TILE), BF16)

    return pl.pallas_call(
        epochs_kernel,
        out_shape=[jax.ShapeDtypeStruct(users.shape, F32), jax.ShapeDtypeStruct(users.shape, F32)],
        in_specs=[smem] * 2 + [anywhere] * 6,
        out_specs=[anywhere, anywhere],
        scratch_shapes=[
            pltpu.VMEM(rows.shape, I32),
            pltpu.VMEM(cols.shape, I32),
            pltpu.SMEM(rows.shape, I32),
            pltpu.SMEM(cols.shape, I32),
            pltpu.VMEM((count * LISTS, 128), I32),
            pltpu.SMEM((count * LISTS, 128), I32),
            pltpu.VMEM(users.shape, F32),
            pltpu.VMEM(mask.shape, I32),
            pltpu.VMEM((SLOTS, TILE, TILE), BF16),
            pltpu.VMEM((SLOTS, TILE, TILE), BF16),
            pltpu.VMEM((4, OWNERS, TILE, RANK), F32),
            pltpu.VMEM((OWNERS, TILE, RANK), F32),
            pltpu.VMEM((WAVES, SLOTS + 1, HALF, TILE), F32),
            pltpu.VMEM((USER_TILES, TILE, RANK), BF16),
            pltpu.VMEM((WAVES, USER_TILES, HALF, TILE), BF16),
            pltpu.VMEM((WAVES, OWNERS * WAVE_UNITS, UNIT, TILE), BF16),
            pltpu.VMEM((WAVES, OWNERS * WAVE_UNITS, UNIT, TILE), BF16),
            pltpu.VMEM((WAVES, OWNERS, WAVE_ROWS, TILE), BF16),
            wide(2, PH), wide(2, PH), wide(2, P_ROWS), wide(2, P_ROWS),
            wide(4, Q_ROWS), wide(QH), wide(QH), wide(Q_ROWS), wide(Q_ROWS), wide(P_ROWS),
            pltpu.VMEM((count, 3, RANK, RANK), BF16),
            pltpu.VMEM((count, 3, RANK, RANK), BF16),
            pltpu.VMEM((OWNERS, RANK, TILE), F32),
            pltpu.VMEM((WAVES, WAVE_ROWS, TILE), F32),
            pltpu.VMEM((WAVES, WAVE_UNITS, UNIT, TILE), BF16),
            pltpu.VMEM((WAVES, WAVE_UNITS, UNIT, TILE), BF16),
            pltpu.VMEM(users.shape, F32),
            dma((SLOTS // GROUP,)),
            dma((OWNERS,)),
            dma((8,)),
            dma((COPIES,)),
            dma((COPIES,)),
        ],
        compiler_params=pltpu.CompilerParams(
            collective_id=0, has_side_effects=True, vmem_limit_bytes=62 * 2**20
        ),
        name="epochs",
    )(counts, owner, rows, cols, ratings, mask, users, items)


PIECES = 4


def settle_kernel(a, b, a_out, b_out, a_here, b_here, come, go):
    rows = a.shape[0] // PIECES
    moves = []
    for src, here, dst in ((a, a_here, a_out), (b, b_here, b_out)):
        for k in range(PIECES):
            s, n = pl.ds(k * rows, rows), len(moves)
            moves.append(
                (
                    pltpu.make_async_copy(src.at[s], here.at[s], come.at[n]),
                    pltpu.make_async_copy(here.at[s], dst.at[s], go.at[n]),
                )
            )
    for first, _ in moves:
        first.start()
    for first, second in moves:
        first.wait()
        second.start()
    for _, second in moves:
        second.wait()


def settled(a, b):
    anywhere = pl.BlockSpec(memory_space=pl.ANY)
    dma = pltpu.SemaphoreType.DMA
    return pl.pallas_call(
        settle_kernel,
        out_shape=[jax.ShapeDtypeStruct(a.shape, a.dtype), jax.ShapeDtypeStruct(b.shape, b.dtype)],
        in_specs=[anywhere] * 2,
        out_specs=[anywhere] * 2,
        scratch_shapes=[
            pltpu.VMEM(a.shape, a.dtype),
            pltpu.VMEM(b.shape, b.dtype),
            dma((2 * PIECES,)),
            dma((2 * PIECES,)),
        ],
        name="settle",
    )(a, b)


def local(ratings, row_index, col_index, row_mask, counts, owner_list, user_factors, item_factors):
    count = ratings.shape[0]
    users, items = epochs(
        counts.reshape(count),
        owner_list.reshape(count),
        row_index.reshape(count, SLOTS),
        col_index.reshape(count, SLOTS),
        ratings.reshape(count, SLOTS, TILE, TILE),
        row_mask.reshape(count, SLOTS, TILE),
        user_factors,
        item_factors.reshape(ITEM_TILES, TILE, RANK),
    )
    return settled(users, items)


def solution(mesh):
    in_specs = (
        P(None, "blk", "grp", None, None, None),
        P(None, "blk", "grp", None),
        P(None, "blk", "grp", None),
        P(None, "blk", "grp", None, None),
        P(None, "blk", "grp"),
        P(None, "blk"),
        P(("blk", "grp"), None),
        P("blk", None),
    )
    out_specs = (P(("blk", "grp"), None), P(("blk", "grp"), None))
    return jax.shard_map(local, mesh=mesh, in_specs=in_specs, out_specs=out_specs, check_vma=False)
```

```python
import functools

import jax
import jax.numpy as jnp
from jax import lax
from jax.experimental import pallas as pl
from jax.experimental.pallas import tpu as pltpu
from jax.sharding import PartitionSpec as P

LEARN = 0.004
GRAM = 256.0
RIDGE = 1.0

TILE = 256
RANK = 128
SLOTS = 64
USER_TILES = 8
ITEM_TILES = 64
OWNERS = 8
GROUP = 8
USER_ROWS = USER_TILES * TILE

WAVES = 2
HALF = RANK // WAVES
WAVE_ROWS = 8 * HALF
P_ROWS = 288
Q_ROWS = WAVE_ROWS - P_ROWS
PH, QH = P_ROWS // 2, Q_ROWS // 2
UNIT = 16
TILE_UNITS = HALF // UNIT
WAVE_UNITS = WAVE_ROWS // UNIT


def units(owner, start, rows):
    return pl.ds(owner * WAVE_UNITS + start // UNIT, rows // UNIT)


PREV_COL, PREV_ROW, LAST_COL, LAST_ROW, LISTS = 0, 1, 2, 3, 4

F32, BF16, I32 = jnp.float32, jnp.bfloat16, jnp.int32
MESH = pl.DeviceIdType.MESH
HIGHEST = lax.Precision.HIGHEST


def dot(a, b, ca=1, cb=0, precision=None):
    return lax.dot_general(
        a, b, (((ca,), (cb,)), ((), ())), precision=precision, preferred_element_type=F32
    )


def ridge():
    row = lax.broadcasted_iota(I32, (RANK, RANK), 0)
    col = lax.broadcasted_iota(I32, (RANK, RANK), 1)
    return jnp.where(row == col, RIDGE, 0.0).astype(F32)


def places():
    b, g = lax.axis_index("blk"), lax.axis_index("grp")
    blocks = lax.axis_size("blk")
    x, yh = g % 4, g // 4
    xp, xm, xo, yo = (x + 1) % 4, (x + 3) % 4, (x + 2) % 4, 1 - yh
    x1 = x + 1 - 2 * (x % 2)
    return dict(
        b=b, g=g, x=x, yh=yh, xp=xp, xm=xm, xo=xo, yo=yo,
        to_xp=(b, yh * 4 + xp), to_xm=(b, yh * 4 + xm), to_xo=(b, yh * 4 + xo),
        to_x1=(b, yh * 4 + x1), to_y=(b, yo * 4 + x),
        to_next=((b + 1) % blocks, g), to_last=((b + blocks - 1) % blocks, g),
    )


PEERS = ("to_xp", "to_xm", "to_xo", "to_y", "to_next", "to_last")


def in_steps(count, step, fn):
    if count == step:
        fn(0)
        return

    @pl.loop(0, count // step)
    def _(k):
        fn(pl.multiple_of(k * step, step))


class Copies:
    def __init__(self, send, recv):
        self.send, self.recv, self.used, self.open = send, recv, 0, []

    def start(self, src, dst, to):
        k = self.used
        assert k < COPIES
        self.used += 1
        copy = pltpu.make_async_remote_copy(
            src_ref=src, dst_ref=dst, send_sem=self.send.at[k], recv_sem=self.recv.at[k],
            device_id=to, device_id_type=MESH,
        )
        copy.start()
        self.open.append(copy)
        return copy

    def finish(self):
        for copy in self.open:
            copy.wait_send()
        self.open = []


COPIES = 160

ORDER_0 = (
    "s0", "g0", "t0", "B", "U", "p0", "s1", "P0", "c0", "v0", "U", "f0", "u0", "g1", "I", "n0",
    "p1", "q0", "u1", "t1", "v1", "C0", "H0", "F0", "f1", "P1", "c1", "n1", "q1", "a0", "b0", "U",
    "C1", "H1", "F1", "x0", "a1", "b1", "U", "r0", "x1", "z0", "G", "r1", "W", "l0", "l1", "z1",
    "k0", "k1",
)
ORDER_1 = (
    "s0", "g0", "v0", "B", "s1", "t0", "U", "t1", "U", "p0", "g1", "G", "f0", "U", "n0", "p1",
    "u0", "c0", "P0", "q0", "I", "P1", "f1", "c1", "v1", "U", "C0", "H0", "u1", "n1", "F0", "q1",
    "C1", "F1", "H1", "W", "O",
)


class Sum:
    def __init__(self, copies, w, wave, part, bufs, base, total, newv):
        self.c, self.w, self.wave = copies, w, wave
        self.part = part.at[wave]
        self.bufs = {k: v.at[wave] for k, v in bufs.items()}
        self.base, self.total, self.newv = base, total.at[wave], newv.at[wave]

    def start(self):
        w, c, part, b, xo = self.w, self.c, self.part, self.bufs, self.w["xo"]
        self.rows = (w["yo"], w["yh"])
        self.one_p, self.one_m, self.q, self.two = [], [], {}, [[], []]
        for a in self.rows:
            self.one_p.append(c.start(part.at[a * 4 + xo, pl.ds(0, PH)], b["r1p"].at[a], w["to_xp"]))
            self.one_m.append(c.start(part.at[a * 4 + xo, pl.ds(PH, PH)], b["r1m"].at[a], w["to_xm"]))
        self.send_q("xo")

    def send_q(self, *names):
        w = self.w
        for name in names:
            self.q[name] = self.c.start(
                self.part.at[w["yo"] * 4 + w[name], pl.ds(P_ROWS, Q_ROWS)], self.bufs["rq"].at[w[name]], w["to_y"]
            )

    def send_p(self, k):
        w, c, part, b, a = self.w, self.c, self.part, self.bufs, self.rows[k]
        pa, pb = pl.ds(0, PH), pl.ds(PH, PH)
        self.two[k].append(c.start(part.at[a * 4 + w["xp"], pb], b["r2p"].at[a, pb], w["to_xp"]))
        self.two[k].append(c.start(part.at[a * 4 + w["xm"], pa], b["r2m"].at[a, pa], w["to_xm"]))

    def pass_p(self, k):
        w, c, part, b, a = self.w, self.c, self.part, self.bufs, self.rows[k]
        xp, xm = w["xp"], w["xm"]
        self.one_p[k].wait_recv()

        def fn(at):
            s = pl.ds(at, 48)
            both = b["r1p"][a, s, :].astype(F32) + part[a * 4 + xp, s, :].astype(F32)
            b["r1p"][a, s, :] = both.astype(BF16)

        in_steps(PH, 48, fn)
        self.two[k].append(c.start(b["r1p"].at[a], b["r2p"].at[a, pl.ds(0, PH)], w["to_xp"]))
        self.one_m[k].wait_recv()

        def fn(at):
            s, t = pl.ds(at, 48), pl.ds(at + PH, 48)
            both = b["r1m"][a, s, :].astype(F32) + part[a * 4 + xm, t, :].astype(F32)
            b["r1m"][a, s, :] = both.astype(BF16)

        in_steps(PH, 48, fn)
        self.two[k].append(c.start(b["r1m"].at[a], b["r2m"].at[a, pl.ds(PH, PH)], w["to_xm"]))

    def add_q(self, copy, d):
        part, b, yh = self.part, self.bufs, self.w["yh"]
        copy.wait_recv()

        def fn(k):
            s, t = pl.ds(k, 112), pl.ds(k + P_ROWS, 112)
            both = b["rq"][d, s, :].astype(F32) + part[yh * 4 + d, t, :].astype(F32)
            b["rq"][d, s, :] = both.astype(BF16)

        in_steps(Q_ROWS, 112, fn)

    def far_q(self):
        w, c, b, xo = self.w, self.c, self.bufs, self.w["xo"]
        self.add_q(self.q["xo"], xo)
        self.q1p = c.start(b["rq"].at[xo, pl.ds(0, QH)], b["q1p"], w["to_xp"])
        self.q1m = c.start(b["rq"].at[xo, pl.ds(QH, QH)], b["q1m"], w["to_xm"])

    def near_q(self):
        w, c, b, xp, xm = self.w, self.c, self.bufs, self.w["xp"], self.w["xm"]
        qa, qb = pl.ds(0, QH), pl.ds(QH, QH)
        self.add_q(self.q["xp"], xp)
        self.q2 = [c.start(b["rq"].at[xp, qb], b["q2p"].at[qb], w["to_xp"])]
        self.add_q(self.q["xm"], xm)
        self.q2.append(c.start(b["rq"].at[xm, qa], b["q2m"].at[qa], w["to_xm"]))

    def pass_q(self):
        w, c, b, xp, xm = self.w, self.c, self.bufs, self.w["xp"], self.w["xm"]
        self.q1p.wait_recv()
        b["q1p"][...] = (b["q1p"][...].astype(F32) + b["rq"][xp, pl.ds(0, QH), :].astype(F32)).astype(BF16)
        self.q2.append(c.start(b["q1p"], b["q2p"].at[pl.ds(0, QH)], w["to_xp"]))
        self.q1m.wait_recv()
        b["q1m"][...] = (b["q1m"][...].astype(F32) + b["rq"][xm, pl.ds(QH, QH), :].astype(F32)).astype(BF16)
        self.q2.append(c.start(b["q1m"], b["q2m"].at[pl.ds(QH, QH)], w["to_xm"]))

    def sum_p(self, a, s):
        part, b = self.part, self.bufs
        both = b["r2p"][a, s, :].astype(F32) + b["r2m"][a, s, :].astype(F32)
        return both + part[a * 4 + self.w["x"], s, :].astype(F32)

    def cross_p(self):
        w, b, yo = self.w, self.bufs, self.w["yo"]
        for copy in self.two[0]:
            copy.wait_recv()

        def fn(k):
            s = pl.ds(k, 48)
            b["r2p"][yo, s, :] = self.sum_p(yo, s).astype(BF16)

        in_steps(P_ROWS, 48, fn)
        self.y = self.c.start(b["r2p"].at[yo], b["ry"], w["to_y"])

    def keep_p(self):
        yh = self.w["yh"]
        for copy in self.two[1]:
            copy.wait_recv()

        def fn(k):
            s = pl.ds(k, 48)
            self.total[s, :] = self.sum_p(yh, s)

        in_steps(P_ROWS, 48, fn)

    def update(self, start, rows, grad, landing):
        @pl.loop(0, rows // 32)
        def _(k):
            at = start // 32 + k
            col = pl.multiple_of(lax.rem(at, 2) * 32, 32) + HALF * self.wave
            old = self.base[lax.div(at, 2), pl.ds(col, 32), :]
            new = (old - LEARN * grad(pl.multiple_of(k * 32, 32))).astype(BF16)
            self.newv[at * 2] = new[:UNIT]
            self.newv[at * 2 + 1] = new[UNIT:]

        place, owner = landing
        return self.c.start(
            self.newv.at[units(0, start, rows)], place.at[self.wave].at[units(owner, start, rows)], self.w["to_next"]
        )

    def finish_q(self, landing):
        b, x = self.bufs, self.w["x"]
        self.add_q(self.q["x"], x)
        for copy in self.q2:
            copy.wait_recv()

        def grad(k):
            s = pl.ds(k, 32)
            both = b["q2p"][s, :].astype(F32) + b["q2m"][s, :].astype(F32)
            return b["rq"][x, s, :].astype(F32) + both

        self.shift_q = self.update(P_ROWS, Q_ROWS, grad, landing)

    def finish_p(self, landing):
        self.y.wait_recv()

        def grad(k):
            s = pl.ds(k, 32)
            return self.total[s, :] + self.bufs["ry"][s, :].astype(F32)

        self.shift_p = self.update(0, P_ROWS, grad, landing)


class Gather:
    def __init__(self, copies, w, wave, vt):
        self.c, self.w, self.vt = copies, w, vt.at[wave]

    def along(self, owner, rows, to):
        ref = self.vt.at[units(owner, *rows)]
        return self.c.start(ref, ref, self.w[to])

    def first(self, one):
        me = self.w["g"]
        p = (0, P_ROWS)
        one.shift_p.wait_recv()
        self.py = self.along(me, p, "to_y")
        self.pp = [self.along(me, p, "to_xp")]
        self.pm = [self.along(me, p, "to_xm")]

    def first_q(self, one):
        me, q = self.w["g"], (P_ROWS, Q_ROWS)
        one.shift_q.wait_recv()
        self.qp = self.along(me, q, "to_xp")
        self.qm = self.along(me, q, "to_xm")
        self.rest = [self.along(me, q, "to_y")]

    def across(self):
        w = self.w
        self.py.wait_recv()
        p = (0, P_ROWS)
        self.pp.append(self.along(w["yo"] * 4 + w["x"], p, "to_xp"))
        self.pm.append(self.along(w["yo"] * 4 + w["x"], p, "to_xm"))

    def forward_p(self, k):
        w = self.w
        row = (w["yh"], w["yo"])[k] * 4
        self.pp[k].wait_recv()
        self.rest.append(self.along(row + w["xm"], (0, PH), "to_xp"))
        self.pm[k].wait_recv()
        self.rest.append(self.along(row + w["xp"], (PH, PH), "to_xm"))

    def forward_q(self):
        w = self.w
        row, q = w["yh"] * 4, (P_ROWS, Q_ROWS)
        self.qp.wait_recv()
        self.qf = [self.along(row + w["xm"], (P_ROWS, QH), "to_xp")]
        self.rest.append(self.along(row + w["xm"], q, "to_y"))
        self.qm.wait_recv()
        self.qf.append(self.along(row + w["xp"], (P_ROWS + QH, QH), "to_xm"))
        self.rest.append(self.along(row + w["xp"], q, "to_y"))

    def across_q(self):
        w = self.w
        for copy in self.qf:
            copy.wait_recv()
        self.rest.append(self.along(w["yh"] * 4 + w["xo"], (P_ROWS, Q_ROWS), "to_y"))

    def finish(self):
        for copy in self.rest:
            copy.wait_recv()


def chains(keys, count):
    lane = lax.broadcasted_iota(I32, (SLOTS, SLOTS), 1)
    slot = lax.broadcasted_iota(I32, (SLOTS, SLOTS), 0)
    across = jnp.broadcast_to(keys, (SLOTS, SLOTS))
    down = jnp.sum(jnp.where(lane == slot, across, 0), axis=1, keepdims=True)
    live = slot < count

    def latest(where):
        found = jnp.max(jnp.where(where & live, slot, -1), axis=0, keepdims=True)
        return jnp.where(found < 0, SLOTS, found)

    return latest((down == across) & (slot < lane)), latest(down == lane)


def epochs_kernel(
    counts, owner, rows_in, cols_in, ratings, mask_in, users_in, items_in, users_out, items_out,
    rows_v, cols_v, rows_s, cols_s, lists, idx, users, mask, rbuf, err, stage, vown, acc, ub, ubt, vt0, vt1, part,
    r1p, r1m, r2p, r2m, rq, q1p, q1m, q2p, q2m, ry, gsend, grecv, base, total, newv, landing, final,
    rsem, vsem, lsem, send, recv,
):
    w = places()
    copies = Copies(send, recv)
    chunks = SLOTS // GROUP
    stages = stage.shape[0]
    barrier = pltpu.get_barrier_semaphore()
    for peer in PEERS:
        pl.semaphore_signal(barrier, inc=1, device_id=w[peer], device_id_type=MESH)

    def local_copy(src, dst, k):
        copy = pltpu.make_async_copy(src, dst, lsem.at[k])
        copy.start()
        return copy

    lists_in = [
        local_copy(a, b, 3 + k)
        for k, (a, b) in enumerate(((cols_in, cols_v), (rows_in, rows_v), (cols_in, cols_s), (rows_in, rows_s)))
    ]
    users_here = local_copy(users_in, users, 0)

    def items_here(k):
        copy = pltpu.make_async_copy(
            items_in.at[pl.ds(k * OWNERS, OWNERS)], stage.at[k % stages], vsem.at[k]
        )
        copy.start()
        return copy

    arriving = [items_here(k) for k in range(stages)]
    mask_here = local_copy(mask_in, mask, 1)

    def fetch(e, k):
        s = pl.ds(k * GROUP, GROUP)
        return pltpu.make_async_copy(ratings.at[e, s], rbuf.at[s], rsem.at[k])

    def prepare_users(e, first):
        own = jnp.zeros((RANK, RANK), F32)
        for i in range(USER_TILES):
            u = users[pl.ds(i * TILE, TILE), :]
            ub[i] = u.astype(BF16)
            ut = u.T.astype(BF16)
            ubt[0, i], ubt[1, i] = ut[:HALF], ut[HALF:]
            own = own + dot(ut, ub[i])
        own = (own * (GRAM / USER_ROWS) + ridge()).astype(BF16)
        gsend[e, 0] = jnp.where(owner[e] == w["g"], own, jnp.zeros_like(own))
        if first:
            pl.semaphore_wait(barrier, len(PEERS))
        return copies.start(gsend.at[e, 0], grecv.at[e, 0], w["to_y"])

    def spread_gram(e, k, copy):
        copy.wait_recv()
        gsend[e, k] = gsend[e, k - 1] + grecv[e, k - 1]
        return copies.start(gsend.at[e, k], grecv.at[e, k], w["to_x1" if k == 1 else "to_xo"])

    def vtile(vt, j):
        first = j * TILE_UNITS
        return jnp.concatenate(
            [vt[wave, first + u] for wave in range(WAVES) for u in range(TILE_UNITS)], axis=0
        )

    def weights(e, t):
        row = mask[e, pl.ds(t, 1), :].astype(F32)
        return jnp.where(t < counts[e], row, jnp.zeros_like(row))

    def errors(e, vt, t):
        predicted = dot(ub[rows_s[e, t]], vtile(vt, cols_s[e, t]))
        err[t] = (predicted - rbuf[t].astype(F32)).astype(BF16)

    def item_dot(e, wave, t):
        u = ubt[wave, rows_s[e, t]]
        return dot(u * weights(e, t).astype(BF16), err[t])

    def item_add(e, wave, t, add):
        acc[wave, t] = acc[wave, idx[e * LISTS + PREV_COL, t]] + add

    def item_done(e, wave):
        @pl.loop(0, ITEM_TILES, unroll=4)
        def _(j):
            s = pl.ds(pl.multiple_of(lax.rem(j, OWNERS) * HALF, HALF), HALF)
            part[wave, lax.div(j, OWNERS), s, :] = acc[wave, idx[e * LISTS + LAST_COL, j]].astype(BF16)

    def first_pass(e, vt):
        fetch(e, 0).wait()
        for q in range(GROUP):
            errors(e, vt, q)

        @pl.loop(0, chunks - 1)
        def _(g):
            adds = [item_dot(e, 0, g * GROUP + q) for q in range(GROUP)]
            fetch(e, g + 1).wait()
            for q in range(GROUP):
                errors(e, vt, (g + 1) * GROUP + q)
            for q in range(GROUP):
                item_add(e, 0, g * GROUP + q, adds[q])

        adds = [item_dot(e, 0, SLOTS - GROUP + q) for q in range(GROUP)]
        for q in range(GROUP):
            item_add(e, 0, SLOTS - GROUP + q, adds[q])
        item_done(e, 0)

    def second_pass(e):
        @pl.loop(0, chunks)
        def _(g):
            adds = [item_dot(e, 1, g * GROUP + q) for q in range(GROUP)]
            for q in range(GROUP):
                item_add(e, 1, g * GROUP + q, adds[q])

        item_done(e, 1)

    def user_pass(e, vt, first, last):
        @pl.loop(first, last)
        def _(g):
            def add_dot(t):
                return dot(vtile(vt, cols_s[e, t]), err[t], 1, 1) * weights(e, t)

            for h in range(2):
                slots = [g * GROUP + h * (GROUP // 2) + q for q in range(GROUP // 2)]
                adds = [add_dot(t) for t in slots]
                for t, add in zip(slots, adds):
                    before = idx[e * LISTS + PREV_ROW, t]
                    acc[0, t] = acc[0, before] + add[:HALF]
                    acc[1, t] = acc[1, before] + add[HALF:]

    def item_gram(vt):
        def add(j, gram):
            for q in range(4):
                v = vtile(vt, j * 4 + q)
                gram = gram + dot(v, v, 1, 1)
            return gram

        gram = lax.fori_loop(0, ITEM_TILES // 4, add, jnp.zeros((RANK, RANK), F32))
        return gram * (GRAM / (ITEM_TILES * TILE)) + ridge()

    def user_update(e, pull):
        @pl.loop(0, USER_TILES)
        def _(i):
            s = pl.ds(pl.multiple_of(i * TILE, TILE), TILE)
            u = users[s, :]
            at = idx[e * LISTS + LAST_ROW, i]
            grad = jnp.concatenate([acc[0, at], acc[1, at]], axis=0)
            users[s, :] = u - LEARN * (grad.T + dot(u, pull, precision=HIGHEST))

    def item_base(e, copy):
        copy.wait_recv()
        if e == 0:
            own_here.wait()
        pull = (gsend[e, 2] + grecv[e, 2]).astype(F32)

        @pl.loop(0, OWNERS)
        def _(k):
            if e == 0:
                v = vown[k].T
            else:
                v = vtile(vt1, w["g"] * OWNERS + k).astype(F32)
            base[k] = v - LEARN * dot(pull, v, 0, 0, precision=HIGHEST)

    bufs = dict(
        r1p=r1p, r1m=r1m, r2p=r2p, r2m=r2m, rq=rq, q1p=q1p, q1m=q1m, q2p=q2p, q2m=q2m, ry=ry
    )

    def sums(e):
        at = {k: v.at[e] for k, v in bufs.items()}
        return [Sum(copies, w, wave, part, at, base, total, newv) for wave in range(WAVES)]

    for copy in lists_in:
        copy.wait()
    for e in range(ratings.shape[0]):
        for k, keys in enumerate((cols_v, rows_v)):
            prev, final_slot = chains(keys[e : e + 1, :], counts[e])
            at = e * LISTS + k
            lists[at : at + 1, 0:SLOTS] = prev
            lists[at + 2 : at + 3, 0:SLOTS] = final_slot
    lists_out = local_copy(lists, idx, 7)
    users_here.wait()
    gram_copy = prepare_users(0, True)
    zero = jnp.zeros((HALF, TILE), F32)
    acc[0, SLOTS] = zero
    acc[1, SLOTS] = zero
    for k in range(OWNERS):
        arriving[k].wait()

        @pl.loop(0, OWNERS, unroll=2)
        def _(j):
            v = stage[k % stages, j].T.astype(BF16)
            for u in range(TILE_UNITS):
                at = (k * OWNERS + j) * TILE_UNITS + u
                vt0[0, at] = v[u * UNIT : (u + 1) * UNIT]
                vt0[1, at] = v[HALF + u * UNIT : HALF + (u + 1) * UNIT]

        if k + stages < OWNERS:
            arriving.append(items_here(k + stages))
        for c in range(2 * (k - OWNERS // 2), 2 * (k - OWNERS // 2) + 2):
            if c >= 0:
                fetch(0, c).start()
    gram_copy = spread_gram(0, 1, gram_copy)
    mask_here.wait()
    lists_out.wait()
    own_here = local_copy(items_in.at[pl.ds(w["g"] * OWNERS, OWNERS)], vown, 2)

    def steps(e, vt, landing, gather):
        waves = sums(e)
        table = {}
        for k, one in enumerate(waves):
            table.update({
                "s%d" % k: one.start, "g%d" % k: functools.partial(one.send_q, "xp", "xm"),
                "u%d" % k: functools.partial(one.send_q, "x"), "t%d" % k: functools.partial(one.send_p, 0),
                "v%d" % k: functools.partial(one.send_p, 1), "p%d" % k: functools.partial(one.pass_p, 0),
                "P%d" % k: functools.partial(one.pass_p, 1), "f%d" % k: one.far_q, "n%d" % k: one.near_q,
                "q%d" % k: one.pass_q, "c%d" % k: one.cross_p, "C%d" % k: one.keep_p,
                "F%d" % k: functools.partial(one.finish_p, landing), "H%d" % k: functools.partial(one.finish_q, landing),
            })
            if gather is not None:
                to = Gather(copies, w, k, gather)
                table.update({
                    "a%d" % k: functools.partial(to.first, one), "b%d" % k: functools.partial(to.first_q, one), "x%d" % k: to.across,
                    "k%d" % k: functools.partial(to.forward_p, 0), "r%d" % k: to.forward_q,
                    "l%d" % k: functools.partial(to.forward_p, 1), "z%d" % k: to.across_q, "e%d" % k: to.finish,
                })
        done = [0]

        def some_users():
            user_pass(e, vt, done[0], done[0] + 2)
            done[0] += 2

        table.update(B=functools.partial(second_pass, e), U=some_users)
        pull = []
        table["G"] = lambda: pull.append(item_gram(vt))
        table["W"] = lambda: user_update(e, pull[0])
        return waves, table

    first_pass(0, vt0)
    gram_copy = spread_gram(0, 2, gram_copy)
    waves, table = steps(0, vt0, (vt1, w["g"]), vt1)
    table["I"] = lambda: item_base(0, gram_copy)
    for k in range(chunks):
        fetch(1, k).start()
    for step in ORDER_0:
        table[step]()
    gram_copy = prepare_users(1, False)
    table["e0"]()
    gram_copy = spread_gram(1, 1, gram_copy)
    table["e1"]()
    copies.finish()

    first_pass(1, vt1)
    gram_copy = spread_gram(1, 2, gram_copy)
    waves, table = steps(1, vt1, (landing, 0), None)
    table["I"] = lambda: item_base(1, gram_copy)
    sent = []
    table["O"] = lambda: sent.append(local_copy(users, users_out, 0))
    for step in ORDER_1:
        table[step]()
    users_gone = sent[0]
    for one in waves:
        one.shift_p.wait_recv()
        one.shift_q.wait_recv()

    @pl.loop(0, OWNERS)
    def _(k):
        v = vtile(landing, k).astype(F32)
        final[pl.ds(pl.multiple_of(k * TILE, TILE), TILE), :] = v.T

    items_gone = local_copy(final, items_out, 1)
    copies.finish()
    users_gone.wait()
    items_gone.wait()


def epochs(counts, owner, rows, cols, ratings, mask, users, items):
    smem = pl.BlockSpec(memory_space=pltpu.SMEM)
    anywhere = pl.BlockSpec(memory_space=pl.ANY)
    dma = pltpu.SemaphoreType.DMA
    count = ratings.shape[0]

    def wide(*rows):
        return pltpu.VMEM((count, WAVES, *rows, TILE), BF16)

    return pl.pallas_call(
        epochs_kernel,
        out_shape=[jax.ShapeDtypeStruct(users.shape, F32), jax.ShapeDtypeStruct(users.shape, F32)],
        in_specs=[smem] * 2 + [anywhere] * 6,
        out_specs=[anywhere, anywhere],
        scratch_shapes=[
            pltpu.VMEM(rows.shape, I32),
            pltpu.VMEM(cols.shape, I32),
            pltpu.SMEM(rows.shape, I32),
            pltpu.SMEM(cols.shape, I32),
            pltpu.VMEM((count * LISTS, 128), I32),
            pltpu.SMEM((count * LISTS, 128), I32),
            pltpu.VMEM(users.shape, F32),
            pltpu.VMEM(mask.shape, I32),
            pltpu.VMEM((SLOTS, TILE, TILE), BF16),
            pltpu.VMEM((SLOTS, TILE, TILE), BF16),
            pltpu.VMEM((4, OWNERS, TILE, RANK), F32),
            pltpu.VMEM((OWNERS, TILE, RANK), F32),
            pltpu.VMEM((WAVES, SLOTS + 1, HALF, TILE), F32),
            pltpu.VMEM((USER_TILES, TILE, RANK), BF16),
            pltpu.VMEM((WAVES, USER_TILES, HALF, TILE), BF16),
            pltpu.VMEM((WAVES, OWNERS * WAVE_UNITS, UNIT, TILE), BF16),
            pltpu.VMEM((WAVES, OWNERS * WAVE_UNITS, UNIT, TILE), BF16),
            pltpu.VMEM((WAVES, OWNERS, WAVE_ROWS, TILE), BF16),
            wide(2, PH), wide(2, PH), wide(2, P_ROWS), wide(2, P_ROWS),
            wide(4, Q_ROWS), wide(QH), wide(QH), wide(Q_ROWS), wide(Q_ROWS), wide(P_ROWS),
            pltpu.VMEM((count, 3, RANK, RANK), BF16),
            pltpu.VMEM((count, 3, RANK, RANK), BF16),
            pltpu.VMEM((OWNERS, RANK, TILE), F32),
            pltpu.VMEM((WAVES, P_ROWS, TILE), F32),
            pltpu.VMEM((WAVES, WAVE_UNITS, UNIT, TILE), BF16),
            pltpu.VMEM((WAVES, WAVE_UNITS, UNIT, TILE), BF16),
            pltpu.VMEM(users.shape, F32),
            dma((SLOTS // GROUP,)),
            dma((OWNERS,)),
            dma((8,)),
            dma((COPIES,)),
            dma((COPIES,)),
        ],
        compiler_params=pltpu.CompilerParams(
            collective_id=0, has_side_effects=True, vmem_limit_bytes=62 * 2**20
        ),
        name="epochs",
    )(counts, owner, rows, cols, ratings, mask, users, items)


PIECES = 4


def settle_kernel(a, b, a_out, b_out, a_here, b_here, come, go):
    rows = a.shape[0] // PIECES
    moves = []
    for src, here, dst in ((a, a_here, a_out), (b, b_here, b_out)):
        for k in range(PIECES):
            s, n = pl.ds(k * rows, rows), len(moves)
            moves.append(
                (
                    pltpu.make_async_copy(src.at[s], here.at[s], come.at[n]),
                    pltpu.make_async_copy(here.at[s], dst.at[s], go.at[n]),
                )
            )
    for first, _ in moves:
        first.start()
    for first, second in moves:
        first.wait()
        second.start()
    for _, second in moves:
        second.wait()


def settled(a, b):
    anywhere = pl.BlockSpec(memory_space=pl.ANY)
    dma = pltpu.SemaphoreType.DMA
    return pl.pallas_call(
        settle_kernel,
        out_shape=[jax.ShapeDtypeStruct(a.shape, a.dtype), jax.ShapeDtypeStruct(b.shape, b.dtype)],
        in_specs=[anywhere] * 2,
        out_specs=[anywhere] * 2,
        scratch_shapes=[
            pltpu.VMEM(a.shape, a.dtype),
            pltpu.VMEM(b.shape, b.dtype),
            dma((2 * PIECES,)),
            dma((2 * PIECES,)),
        ],
        name="settle",
    )(a, b)


def local(ratings, row_index, col_index, row_mask, counts, owner_list, user_factors, item_factors):
    count = ratings.shape[0]
    users, items = epochs(
        counts.reshape(count),
        owner_list.reshape(count),
        row_index.reshape(count, SLOTS),
        col_index.reshape(count, SLOTS),
        ratings.reshape(count, SLOTS, TILE, TILE),
        row_mask.reshape(count, SLOTS, TILE),
        user_factors,
        item_factors.reshape(ITEM_TILES, TILE, RANK),
    )
    return settled(users, items)


def solution(mesh):
    in_specs = (
        P(None, "blk", "grp", None, None, None),
        P(None, "blk", "grp", None),
        P(None, "blk", "grp", None),
        P(None, "blk", "grp", None, None),
        P(None, "blk", "grp"),
        P(None, "blk"),
        P(("blk", "grp"), None),
        P("blk", None),
    )
    out_specs = (P(("blk", "grp"), None), P(("blk", "grp"), None))
    return jax.shard_map(local, mesh=mesh, in_specs=in_specs, out_specs=out_specs, check_vma=False)
```

```python
import functools

import jax
import jax.numpy as jnp
from jax import lax
from jax.experimental import pallas as pl
from jax.experimental.pallas import tpu as pltpu
from jax.sharding import PartitionSpec as P

LEARN = 0.004
GRAM = 256.0
RIDGE = 1.0

TILE = 256
RANK = 128
SLOTS = 64
USER_TILES = 8
ITEM_TILES = 64
OWNERS = 8
GROUP = 8
USER_ROWS = USER_TILES * TILE

WAVES = 2
HALF = RANK // WAVES
WAVE_ROWS = 8 * HALF
P_ROWS = 288
Q_ROWS = WAVE_ROWS - P_ROWS
PH, QH = P_ROWS // 2, Q_ROWS // 2
UNIT = 16
TILE_UNITS = HALF // UNIT
WAVE_UNITS = WAVE_ROWS // UNIT


def units(owner, start, rows):
    return pl.ds(owner * WAVE_UNITS + start // UNIT, rows // UNIT)


PREV_COL, PREV_ROW, LAST_COL, LAST_ROW, LISTS = 0, 1, 2, 3, 4

F32, BF16, I32 = jnp.float32, jnp.bfloat16, jnp.int32
MESH = pl.DeviceIdType.MESH
HIGHEST = lax.Precision.HIGHEST


def dot(a, b, ca=1, cb=0, precision=None):
    return lax.dot_general(
        a, b, (((ca,), (cb,)), ((), ())), precision=precision, preferred_element_type=F32
    )


def ridge():
    row = lax.broadcasted_iota(I32, (RANK, RANK), 0)
    col = lax.broadcasted_iota(I32, (RANK, RANK), 1)
    return jnp.where(row == col, RIDGE, 0.0).astype(F32)


def places():
    b, g = lax.axis_index("blk"), lax.axis_index("grp")
    blocks = lax.axis_size("blk")
    x, yh = g % 4, g // 4
    xp, xm, xo, yo = (x + 1) % 4, (x + 3) % 4, (x + 2) % 4, 1 - yh
    x1 = x + 1 - 2 * (x % 2)
    return dict(
        b=b, g=g, x=x, yh=yh, xp=xp, xm=xm, xo=xo, yo=yo,
        to_xp=(b, yh * 4 + xp), to_xm=(b, yh * 4 + xm), to_xo=(b, yh * 4 + xo),
        to_x1=(b, yh * 4 + x1), to_y=(b, yo * 4 + x),
        to_next=((b + 1) % blocks, g), to_last=((b + blocks - 1) % blocks, g),
    )


PEERS = ("to_xp", "to_xm", "to_xo", "to_y", "to_next", "to_last")


def in_steps(count, step, fn):
    if count == step:
        fn(0)
        return

    @pl.loop(0, count // step)
    def _(k):
        fn(pl.multiple_of(k * step, step))


class Copies:
    def __init__(self, send, recv):
        self.send, self.recv, self.used, self.open = send, recv, 0, []

    def start(self, src, dst, to):
        k = self.used
        assert k < COPIES
        self.used += 1
        copy = pltpu.make_async_remote_copy(
            src_ref=src, dst_ref=dst, send_sem=self.send.at[k], recv_sem=self.recv.at[k],
            device_id=to, device_id_type=MESH,
        )
        copy.start()
        self.open.append(copy)
        return copy

    def finish(self):
        for copy in self.open:
            copy.wait_send()
        self.open = []


COPIES = 160

ORDER_0 = (
    "s0", "g0", "t0", "B", "U", "p0", "s1", "P0", "c0", "v0", "U", "f0", "u0", "g1", "I", "n0",
    "p1", "q0", "u1", "t1", "v1", "C0", "H0", "F0", "f1", "P1", "c1", "n1", "q1", "a0", "b0", "U",
    "C1", "H1", "F1", "x0", "a1", "b1", "U", "r0", "x1", "z0", "G", "r1", "W", "l0", "l1", "z1",
    "k0", "k1",
)
ORDER_1 = (
    "s0", "g0", "v0", "B", "s1", "t0", "U", "t1", "U", "p0", "g1", "G", "f0", "U", "n0", "p1",
    "u0", "c0", "P0", "q0", "I", "P1", "f1", "c1", "v1", "U", "C0", "H0", "u1", "n1", "F0", "q1",
    "C1", "F1", "H1", "W", "O",
)


class Sum:
    def __init__(self, copies, w, wave, part, bufs, base, total, newv):
        self.c, self.w, self.wave = copies, w, wave
        self.part = part.at[wave]
        self.bufs = {k: v.at[wave] for k, v in bufs.items()}
        self.base, self.total, self.newv = base, total.at[wave], newv.at[wave]

    def start(self):
        w, c, part, b, xo = self.w, self.c, self.part, self.bufs, self.w["xo"]
        self.rows = (w["yo"], w["yh"])
        self.one_p, self.one_m, self.q, self.two = [], [], {}, [[], []]
        for a in self.rows:
            self.one_p.append(c.start(part.at[a * 4 + xo, pl.ds(0, PH)], b["r1p"].at[a], w["to_xp"]))
            self.one_m.append(c.start(part.at[a * 4 + xo, pl.ds(PH, PH)], b["r1m"].at[a], w["to_xm"]))
        self.send_q("xo")

    def send_q(self, *names):
        w = self.w
        for name in names:
            self.q[name] = self.c.start(
                self.part.at[w["yo"] * 4 + w[name], pl.ds(P_ROWS, Q_ROWS)], self.bufs["rq"].at[w[name]], w["to_y"]
            )

    def send_p(self, k):
        w, c, part, b, a = self.w, self.c, self.part, self.bufs, self.rows[k]
        pa, pb = pl.ds(0, PH), pl.ds(PH, PH)
        self.two[k].append(c.start(part.at[a * 4 + w["xp"], pb], b["r2p"].at[a, pb], w["to_xp"]))
        self.two[k].append(c.start(part.at[a * 4 + w["xm"], pa], b["r2m"].at[a, pa], w["to_xm"]))

    def pass_p(self, k):
        w, c, part, b, a = self.w, self.c, self.part, self.bufs, self.rows[k]
        xp, xm = w["xp"], w["xm"]
        self.one_p[k].wait_recv()

        def fn(at):
            s = pl.ds(at, 48)
            both = b["r1p"][a, s, :].astype(F32) + part[a * 4 + xp, s, :].astype(F32)
            b["r1p"][a, s, :] = both.astype(BF16)

        in_steps(PH, 48, fn)
        self.two[k].append(c.start(b["r1p"].at[a], b["r2p"].at[a, pl.ds(0, PH)], w["to_xp"]))
        self.one_m[k].wait_recv()

        def fn(at):
            s, t = pl.ds(at, 48), pl.ds(at + PH, 48)
            both = b["r1m"][a, s, :].astype(F32) + part[a * 4 + xm, t, :].astype(F32)
            b["r1m"][a, s, :] = both.astype(BF16)

        in_steps(PH, 48, fn)
        self.two[k].append(c.start(b["r1m"].at[a], b["r2m"].at[a, pl.ds(PH, PH)], w["to_xm"]))

    def add_q(self, copy, d):
        part, b, yh = self.part, self.bufs, self.w["yh"]
        copy.wait_recv()

        def fn(k):
            s, t = pl.ds(k, 112), pl.ds(k + P_ROWS, 112)
            both = b["rq"][d, s, :].astype(F32) + part[yh * 4 + d, t, :].astype(F32)
            b["rq"][d, s, :] = both.astype(BF16)

        in_steps(Q_ROWS, 112, fn)

    def far_q(self):
        w, c, b, xo = self.w, self.c, self.bufs, self.w["xo"]
        self.add_q(self.q["xo"], xo)
        self.q1p = c.start(b["rq"].at[xo, pl.ds(0, QH)], b["q1p"], w["to_xp"])
        self.q1m = c.start(b["rq"].at[xo, pl.ds(QH, QH)], b["q1m"], w["to_xm"])

    def near_q(self):
        w, c, b, xp, xm = self.w, self.c, self.bufs, self.w["xp"], self.w["xm"]
        qa, qb = pl.ds(0, QH), pl.ds(QH, QH)
        self.add_q(self.q["xp"], xp)
        self.q2 = [c.start(b["rq"].at[xp, qb], b["q2p"].at[qb], w["to_xp"])]
        self.add_q(self.q["xm"], xm)
        self.q2.append(c.start(b["rq"].at[xm, qa], b["q2m"].at[qa], w["to_xm"]))

    def pass_q(self):
        w, c, b, xp, xm = self.w, self.c, self.bufs, self.w["xp"], self.w["xm"]
        self.q1p.wait_recv()
        b["q1p"][...] = (b["q1p"][...].astype(F32) + b["rq"][xp, pl.ds(0, QH), :].astype(F32)).astype(BF16)
        self.q2.append(c.start(b["q1p"], b["q2p"].at[pl.ds(0, QH)], w["to_xp"]))
        self.q1m.wait_recv()
        b["q1m"][...] = (b["q1m"][...].astype(F32) + b["rq"][xm, pl.ds(QH, QH), :].astype(F32)).astype(BF16)
        self.q2.append(c.start(b["q1m"], b["q2m"].at[pl.ds(QH, QH)], w["to_xm"]))

    def sum_p(self, a, s):
        part, b = self.part, self.bufs
        both = b["r2p"][a, s, :].astype(F32) + b["r2m"][a, s, :].astype(F32)
        return both + part[a * 4 + self.w["x"], s, :].astype(F32)

    def cross_p(self):
        w, b, yo = self.w, self.bufs, self.w["yo"]
        for copy in self.two[0]:
            copy.wait_recv()

        def fn(k):
            s = pl.ds(k, 48)
            b["r2p"][yo, s, :] = self.sum_p(yo, s).astype(BF16)

        in_steps(P_ROWS, 48, fn)
        self.y = self.c.start(b["r2p"].at[yo], b["ry"], w["to_y"])

    def keep_p(self):
        yh = self.w["yh"]
        for copy in self.two[1]:
            copy.wait_recv()

        def fn(k):
            s = pl.ds(k, 48)
            self.total[s, :] = self.sum_p(yh, s)

        in_steps(P_ROWS, 48, fn)

    def update(self, start, rows, grad, landing):
        @pl.loop(0, rows // 32)
        def _(k):
            at = start // 32 + k
            col = pl.multiple_of(lax.rem(at, 2) * 32, 32) + HALF * self.wave
            old = self.base[lax.div(at, 2), pl.ds(col, 32), :]
            new = (old - LEARN * grad(pl.multiple_of(k * 32, 32))).astype(BF16)
            self.newv[at * 2] = new[:UNIT]
            self.newv[at * 2 + 1] = new[UNIT:]

        place, owner = landing
        return self.c.start(
            self.newv.at[units(0, start, rows)], place.at[self.wave].at[units(owner, start, rows)], self.w["to_next"]
        )

    def finish_q(self, landing):
        b, x = self.bufs, self.w["x"]
        self.add_q(self.q["x"], x)
        for copy in self.q2:
            copy.wait_recv()

        def grad(k):
            s = pl.ds(k, 32)
            both = b["q2p"][s, :].astype(F32) + b["q2m"][s, :].astype(F32)
            return b["rq"][x, s, :].astype(F32) + both

        self.shift_q = self.update(P_ROWS, Q_ROWS, grad, landing)

    def finish_p(self, landing):
        self.y.wait_recv()

        def grad(k):
            s = pl.ds(k, 32)
            return self.total[s, :] + self.bufs["ry"][s, :].astype(F32)

        self.shift_p = self.update(0, P_ROWS, grad, landing)


class Gather:
    def __init__(self, copies, w, wave, vt):
        self.c, self.w, self.vt = copies, w, vt.at[wave]

    def along(self, owner, rows, to):
        ref = self.vt.at[units(owner, *rows)]
        return self.c.start(ref, ref, self.w[to])

    def first(self, one):
        me = self.w["g"]
        p = (0, P_ROWS)
        one.shift_p.wait_recv()
        self.py = self.along(me, p, "to_y")
        self.pp = [self.along(me, p, "to_xp")]
        self.pm = [self.along(me, p, "to_xm")]

    def first_q(self, one):
        me, q = self.w["g"], (P_ROWS, Q_ROWS)
        one.shift_q.wait_recv()
        self.qp = self.along(me, q, "to_xp")
        self.qm = self.along(me, q, "to_xm")
        self.rest = [self.along(me, q, "to_y")]

    def across(self):
        w = self.w
        self.py.wait_recv()
        p = (0, P_ROWS)
        self.pp.append(self.along(w["yo"] * 4 + w["x"], p, "to_xp"))
        self.pm.append(self.along(w["yo"] * 4 + w["x"], p, "to_xm"))

    def forward_p(self, k):
        w = self.w
        row = (w["yh"], w["yo"])[k] * 4
        self.pp[k].wait_recv()
        self.rest.append(self.along(row + w["xm"], (0, PH), "to_xp"))
        self.pm[k].wait_recv()
        self.rest.append(self.along(row + w["xp"], (PH, PH), "to_xm"))

    def forward_q(self):
        w = self.w
        row, q = w["yh"] * 4, (P_ROWS, Q_ROWS)
        self.qp.wait_recv()
        self.qf = [self.along(row + w["xm"], (P_ROWS, QH), "to_xp")]
        self.rest.append(self.along(row + w["xm"], q, "to_y"))
        self.qm.wait_recv()
        self.qf.append(self.along(row + w["xp"], (P_ROWS + QH, QH), "to_xm"))
        self.rest.append(self.along(row + w["xp"], q, "to_y"))

    def across_q(self):
        w = self.w
        for copy in self.qf:
            copy.wait_recv()
        self.rest.append(self.along(w["yh"] * 4 + w["xo"], (P_ROWS, Q_ROWS), "to_y"))

    def finish(self):
        for copy in self.rest:
            copy.wait_recv()


def chains(keys, count):
    lane = lax.broadcasted_iota(I32, (SLOTS, SLOTS), 1)
    slot = lax.broadcasted_iota(I32, (SLOTS, SLOTS), 0)
    across = jnp.broadcast_to(keys, (SLOTS, SLOTS))
    down = jnp.sum(jnp.where(lane == slot, across, 0), axis=1, keepdims=True)
    live = slot < count

    def latest(where):
        found = jnp.max(jnp.where(where & live, slot, -1), axis=0, keepdims=True)
        return jnp.where(found < 0, SLOTS, found)

    return latest((down == across) & (slot < lane)), latest(down == lane)


def epochs_kernel(
    counts, owner, rows_in, cols_in, ratings, mask_in, users_in, items_in, users_out, items_out,
    rows_v, cols_v, rows_s, cols_s, lists, idx, users, mask, rbuf, err, stage, vown, acc, ub, ubt, vt0, vt1, part,
    r1p, r1m, r2p, r2m, rq, q1p, q1m, q2p, q2m, ry, gsend, grecv, base, total, newv, landing, final,
    rsem, vsem, lsem, send, recv,
):
    w = places()
    copies = Copies(send, recv)
    chunks = SLOTS // GROUP
    stages = stage.shape[0]
    barrier = pltpu.get_barrier_semaphore()
    for peer in PEERS:
        pl.semaphore_signal(barrier, inc=1, device_id=w[peer], device_id_type=MESH)

    def local_copy(src, dst, k):
        copy = pltpu.make_async_copy(src, dst, lsem.at[k])
        copy.start()
        return copy

    lists_in = [
        local_copy(a, b, 3 + k)
        for k, (a, b) in enumerate(((cols_in, cols_v), (rows_in, rows_v), (cols_in, cols_s), (rows_in, rows_s)))
    ]
    users_here = local_copy(users_in, users, 0)

    def items_here(k):
        copy = pltpu.make_async_copy(
            items_in.at[pl.ds(k * OWNERS, OWNERS)], stage.at[k % stages], vsem.at[k]
        )
        copy.start()
        return copy

    arriving = [items_here(k) for k in range(stages)]
    mask_here = local_copy(mask_in, mask, 1)

    def fetch(e, k):
        s = pl.ds(k * GROUP, GROUP)
        return pltpu.make_async_copy(ratings.at[e, s], rbuf.at[s], rsem.at[k])

    def prepare_users(e, first):
        own = jnp.zeros((RANK, RANK), F32)
        for i in range(USER_TILES):
            u = users[pl.ds(i * TILE, TILE), :]
            ub[i] = u.astype(BF16)
            ut = u.T.astype(BF16)
            ubt[0, i], ubt[1, i] = ut[:HALF], ut[HALF:]
            own = own + dot(ut, ub[i])
        own = (own * (GRAM / USER_ROWS) + ridge()).astype(BF16)
        gsend[e, 0] = jnp.where(owner[e] == w["g"], own, jnp.zeros_like(own))
        if first:
            pl.semaphore_wait(barrier, len(PEERS))
        return copies.start(gsend.at[e, 0], grecv.at[e, 0], w["to_y"])

    def spread_gram(e, k, copy):
        copy.wait_recv()
        gsend[e, k] = gsend[e, k - 1] + grecv[e, k - 1]
        return copies.start(gsend.at[e, k], grecv.at[e, k], w["to_x1" if k == 1 else "to_xo"])

    def vtile(vt, j):
        first = j * TILE_UNITS
        return jnp.concatenate(
            [vt[wave, first + u] for wave in range(WAVES) for u in range(TILE_UNITS)], axis=0
        )

    def weights(e, t):
        row = mask[e, pl.ds(t, 1), :].astype(F32)
        return jnp.where(t < counts[e], row, jnp.zeros_like(row))

    def errors(e, vt, t):
        predicted = dot(ub[rows_s[e, t]], vtile(vt, cols_s[e, t]))
        err[t] = (predicted - rbuf[t].astype(F32)).astype(BF16)

    def item_dot(e, wave, t):
        u = ubt[wave, rows_s[e, t]]
        return dot(u * weights(e, t).astype(BF16), err[t])

    def item_add(e, wave, t, add):
        acc[wave, t] = acc[wave, idx[e * LISTS + PREV_COL, t]] + add

    def item_done(e, wave):
        @pl.loop(0, ITEM_TILES, unroll=4)
        def _(j):
            s = pl.ds(pl.multiple_of(lax.rem(j, OWNERS) * HALF, HALF), HALF)
            part[wave, lax.div(j, OWNERS), s, :] = acc[wave, idx[e * LISTS + LAST_COL, j]].astype(BF16)

    def first_pass(e, vt):
        fetch(e, 0).wait()
        for q in range(GROUP):
            errors(e, vt, q)

        @pl.loop(0, chunks - 1)
        def _(g):
            adds = [item_dot(e, 0, g * GROUP + q) for q in range(GROUP)]
            fetch(e, g + 1).wait()
            for q in range(GROUP):
                errors(e, vt, (g + 1) * GROUP + q)
            for q in range(GROUP):
                item_add(e, 0, g * GROUP + q, adds[q])

        adds = [item_dot(e, 0, SLOTS - GROUP + q) for q in range(GROUP)]
        for q in range(GROUP):
            item_add(e, 0, SLOTS - GROUP + q, adds[q])
        item_done(e, 0)

    def second_pass(e):
        @pl.loop(0, chunks)
        def _(g):
            adds = [item_dot(e, 1, g * GROUP + q) for q in range(GROUP)]
            for q in range(GROUP):
                item_add(e, 1, g * GROUP + q, adds[q])

        item_done(e, 1)

    def user_pass(e, vt, first, last):
        @pl.loop(first, last)
        def _(g):
            def add_dot(t):
                return dot(vtile(vt, cols_s[e, t]), err[t], 1, 1) * weights(e, t)

            for h in range(2):
                slots = [g * GROUP + h * (GROUP // 2) + q for q in range(GROUP // 2)]
                adds = [add_dot(t) for t in slots]
                for t, add in zip(slots, adds):
                    before = idx[e * LISTS + PREV_ROW, t]
                    acc[0, t] = acc[0, before] + add[:HALF]
                    acc[1, t] = acc[1, before] + add[HALF:]

    def item_gram(vt):
        def add(j, gram):
            for q in range(4):
                v = vtile(vt, j * 4 + q)
                gram = gram + dot(v, v, 1, 1)
            return gram

        gram = lax.fori_loop(0, ITEM_TILES // 4, add, jnp.zeros((RANK, RANK), F32))
        return gram * (GRAM / (ITEM_TILES * TILE)) + ridge()

    def user_update(e, pull):
        @pl.loop(0, USER_TILES)
        def _(i):
            s = pl.ds(pl.multiple_of(i * TILE, TILE), TILE)
            u = users[s, :]
            at = idx[e * LISTS + LAST_ROW, i]
            grad = jnp.concatenate([acc[0, at], acc[1, at]], axis=0)
            users[s, :] = u - LEARN * (grad.T + dot(u, pull, precision=HIGHEST))

    def item_base(e, copy):
        copy.wait_recv()
        if e == 0:
            own_here.wait()
        pull = (gsend[e, 2] + grecv[e, 2]).astype(F32)

        @pl.loop(0, OWNERS)
        def _(k):
            if e == 0:
                v = vown[k].T
            else:
                v = vtile(vt1, w["g"] * OWNERS + k).astype(F32)
            base[k] = v - LEARN * dot(pull, v, 0, 0, precision=HIGHEST)

    bufs = dict(
        r1p=r1p, r1m=r1m, r2p=r2p, r2m=r2m, rq=rq, q1p=q1p, q1m=q1m, q2p=q2p, q2m=q2m, ry=ry
    )

    def sums(e):
        at = {k: v.at[e] for k, v in bufs.items()}
        return [Sum(copies, w, wave, part, at, base, total, newv) for wave in range(WAVES)]

    zero = jnp.zeros((HALF, TILE), F32)
    acc[0, SLOTS] = zero
    acc[1, SLOTS] = zero
    for k in range(OWNERS):
        if k == stages:
            for copy in lists_in:
                copy.wait()
            for e in range(ratings.shape[0]):
                for n, keys in enumerate((cols_v, rows_v)):
                    prev, final_slot = chains(keys[e : e + 1, :], counts[e])
                    at = e * LISTS + n
                    lists[at : at + 1, 0:SLOTS] = prev
                    lists[at + 2 : at + 3, 0:SLOTS] = final_slot
            lists_out = local_copy(lists, idx, 7)
            users_here.wait()
            gram_copy = prepare_users(0, True)
        arriving[k].wait()

        @pl.loop(0, OWNERS, unroll=2)
        def _(j):
            v = stage[k % stages, j].T.astype(BF16)
            for u in range(TILE_UNITS):
                at = (k * OWNERS + j) * TILE_UNITS + u
                vt0[0, at] = v[u * UNIT : (u + 1) * UNIT]
                vt0[1, at] = v[HALF + u * UNIT : HALF + (u + 1) * UNIT]

        if k + stages < OWNERS:
            arriving.append(items_here(k + stages))
        for c in range(2 * (k - OWNERS // 2), 2 * (k - OWNERS // 2) + 2):
            if c >= 0:
                fetch(0, c).start()
    gram_copy = spread_gram(0, 1, gram_copy)
    mask_here.wait()
    lists_out.wait()
    own_here = local_copy(items_in.at[pl.ds(w["g"] * OWNERS, OWNERS)], vown, 2)

    def steps(e, vt, landing, gather):
        waves = sums(e)
        table = {}
        for k, one in enumerate(waves):
            table.update({
                "s%d" % k: one.start, "g%d" % k: functools.partial(one.send_q, "xp", "xm"),
                "u%d" % k: functools.partial(one.send_q, "x"), "t%d" % k: functools.partial(one.send_p, 0),
                "v%d" % k: functools.partial(one.send_p, 1), "p%d" % k: functools.partial(one.pass_p, 0),
                "P%d" % k: functools.partial(one.pass_p, 1), "f%d" % k: one.far_q, "n%d" % k: one.near_q,
                "q%d" % k: one.pass_q, "c%d" % k: one.cross_p, "C%d" % k: one.keep_p,
                "F%d" % k: functools.partial(one.finish_p, landing), "H%d" % k: functools.partial(one.finish_q, landing),
            })
            if gather is not None:
                to = Gather(copies, w, k, gather)
                table.update({
                    "a%d" % k: functools.partial(to.first, one), "b%d" % k: functools.partial(to.first_q, one), "x%d" % k: to.across,
                    "k%d" % k: functools.partial(to.forward_p, 0), "r%d" % k: to.forward_q,
                    "l%d" % k: functools.partial(to.forward_p, 1), "z%d" % k: to.across_q, "e%d" % k: to.finish,
                })
        done = [0]

        def some_users():
            user_pass(e, vt, done[0], done[0] + 2)
            done[0] += 2

        table.update(B=functools.partial(second_pass, e), U=some_users)
        pull = []
        table["G"] = lambda: pull.append(item_gram(vt))
        table["W"] = lambda: user_update(e, pull[0])
        return waves, table

    first_pass(0, vt0)
    gram_copy = spread_gram(0, 2, gram_copy)
    waves, table = steps(0, vt0, (vt1, w["g"]), vt1)
    table["I"] = lambda: item_base(0, gram_copy)
    for k in range(chunks):
        fetch(1, k).start()
    for step in ORDER_0:
        table[step]()
    gram_copy = prepare_users(1, False)
    table["e0"]()
    gram_copy = spread_gram(1, 1, gram_copy)
    table["e1"]()
    copies.finish()

    first_pass(1, vt1)
    gram_copy = spread_gram(1, 2, gram_copy)
    waves, table = steps(1, vt1, (landing, 0), None)
    table["I"] = lambda: item_base(1, gram_copy)
    sent = []
    table["O"] = lambda: sent.append(local_copy(users, users_out, 0))
    for step in ORDER_1:
        table[step]()
    users_gone = sent[0]
    for one in waves:
        one.shift_p.wait_recv()
        one.shift_q.wait_recv()

    @pl.loop(0, OWNERS)
    def _(k):
        v = vtile(landing, k).astype(F32)
        final[pl.ds(pl.multiple_of(k * TILE, TILE), TILE), :] = v.T

    items_gone = local_copy(final, items_out, 1)
    copies.finish()
    users_gone.wait()
    items_gone.wait()


def epochs(counts, owner, rows, cols, ratings, mask, users, items):
    smem = pl.BlockSpec(memory_space=pltpu.SMEM)
    anywhere = pl.BlockSpec(memory_space=pl.ANY)
    dma = pltpu.SemaphoreType.DMA
    count = ratings.shape[0]

    def wide(*rows):
        return pltpu.VMEM((count, WAVES, *rows, TILE), BF16)

    return pl.pallas_call(
        epochs_kernel,
        out_shape=[jax.ShapeDtypeStruct(users.shape, F32), jax.ShapeDtypeStruct(users.shape, F32)],
        in_specs=[smem] * 2 + [anywhere] * 6,
        out_specs=[anywhere, anywhere],
        scratch_shapes=[
            pltpu.VMEM(rows.shape, I32),
            pltpu.VMEM(cols.shape, I32),
            pltpu.SMEM(rows.shape, I32),
            pltpu.SMEM(cols.shape, I32),
            pltpu.VMEM((count * LISTS, 128), I32),
            pltpu.SMEM((count * LISTS, 128), I32),
            pltpu.VMEM(users.shape, F32),
            pltpu.VMEM(mask.shape, I32),
            pltpu.VMEM((SLOTS, TILE, TILE), BF16),
            pltpu.VMEM((SLOTS, TILE, TILE), BF16),
            pltpu.VMEM((4, OWNERS, TILE, RANK), F32),
            pltpu.VMEM((OWNERS, TILE, RANK), F32),
            pltpu.VMEM((WAVES, SLOTS + 1, HALF, TILE), F32),
            pltpu.VMEM((USER_TILES, TILE, RANK), BF16),
            pltpu.VMEM((WAVES, USER_TILES, HALF, TILE), BF16),
            pltpu.VMEM((WAVES, OWNERS * WAVE_UNITS, UNIT, TILE), BF16),
            pltpu.VMEM((WAVES, OWNERS * WAVE_UNITS, UNIT, TILE), BF16),
            pltpu.VMEM((WAVES, OWNERS, WAVE_ROWS, TILE), BF16),
            wide(2, PH), wide(2, PH), wide(2, P_ROWS), wide(2, P_ROWS),
            wide(4, Q_ROWS), wide(QH), wide(QH), wide(Q_ROWS), wide(Q_ROWS), wide(P_ROWS),
            pltpu.VMEM((count, 3, RANK, RANK), BF16),
            pltpu.VMEM((count, 3, RANK, RANK), BF16),
            pltpu.VMEM((OWNERS, RANK, TILE), F32),
            pltpu.VMEM((WAVES, P_ROWS, TILE), F32),
            pltpu.VMEM((WAVES, WAVE_UNITS, UNIT, TILE), BF16),
            pltpu.VMEM((WAVES, WAVE_UNITS, UNIT, TILE), BF16),
            pltpu.VMEM(users.shape, F32),
            dma((SLOTS // GROUP,)),
            dma((OWNERS,)),
            dma((8,)),
            dma((COPIES,)),
            dma((COPIES,)),
        ],
        compiler_params=pltpu.CompilerParams(
            collective_id=0, has_side_effects=True, vmem_limit_bytes=62 * 2**20
        ),
        name="epochs",
    )(counts, owner, rows, cols, ratings, mask, users, items)


PIECES = 4


def settle_kernel(a, b, a_out, b_out, a_here, b_here, come, go):
    rows = a.shape[0] // PIECES
    moves = []
    for src, here, dst in ((a, a_here, a_out), (b, b_here, b_out)):
        for k in range(PIECES):
            s, n = pl.ds(k * rows, rows), len(moves)
            moves.append(
                (
                    pltpu.make_async_copy(src.at[s], here.at[s], come.at[n]),
                    pltpu.make_async_copy(here.at[s], dst.at[s], go.at[n]),
                )
            )
    for first, _ in moves:
        first.start()
    for first, second in moves:
        first.wait()
        second.start()
    for _, second in moves:
        second.wait()


def settled(a, b):
    anywhere = pl.BlockSpec(memory_space=pl.ANY)
    dma = pltpu.SemaphoreType.DMA
    return pl.pallas_call(
        settle_kernel,
        out_shape=[jax.ShapeDtypeStruct(a.shape, a.dtype), jax.ShapeDtypeStruct(b.shape, b.dtype)],
        in_specs=[anywhere] * 2,
        out_specs=[anywhere] * 2,
        scratch_shapes=[
            pltpu.VMEM(a.shape, a.dtype),
            pltpu.VMEM(b.shape, b.dtype),
            dma((2 * PIECES,)),
            dma((2 * PIECES,)),
        ],
        name="settle",
    )(a, b)


def local(ratings, row_index, col_index, row_mask, counts, owner_list, user_factors, item_factors):
    count = ratings.shape[0]
    users, items = epochs(
        counts.reshape(count),
        owner_list.reshape(count),
        row_index.reshape(count, SLOTS),
        col_index.reshape(count, SLOTS),
        ratings.reshape(count, SLOTS, TILE, TILE),
        row_mask.reshape(count, SLOTS, TILE),
        user_factors,
        item_factors.reshape(ITEM_TILES, TILE, RANK),
    )
    return settled(users, items)


def solution(mesh):
    in_specs = (
        P(None, "blk", "grp", None, None, None),
        P(None, "blk", "grp", None),
        P(None, "blk", "grp", None),
        P(None, "blk", "grp", None, None),
        P(None, "blk", "grp"),
        P(None, "blk"),
        P(("blk", "grp"), None),
        P("blk", None),
    )
    out_specs = (P(("blk", "grp"), None), P(("blk", "grp"), None))
    return jax.shard_map(local, mesh=mesh, in_specs=in_specs, out_specs=out_specs, check_vma=False)
```
